512 devices in a mesh: sector: 16 (over z), chan: 32 (over x, y, core).
Axes of the slice: x: 4, y: 4, z: 16, core: 2. Of those that a mesh axis runs over, the one named last changes fastest.
Arguments:
- angular: bfloat16 [2048, 2048], P(None, 'chan'), may hold values from -0.125 to 0.125
- potential: float32 [32, 2048], replicated, may hold values from 0.25 to 4
- point_rows: int32 [32], replicated, may hold values from 0 to 31, each once
- quanta: int32 [2, 2048], P(None, 'chan'), may hold values from 0 to 7
- start_waves: float32 [48, 2048], P(None, 'chan'), may hold values from -6 to 6
Outputs:
- waves: float32 [32, 48, 2048], P('sector', None, 'chan')
The draws below stay inside these ranges and needn't reach their ends.
Inputs may be any that keep to these rules, and one draw needn't show every extreme that they name: `point_rows`: A permutation: each row of potential belongs to exactly one radial point.
All inputs are finite; a program needn't handle non-finite values.
Results may differ from the reference program's by a relative error of at most 0.014.
Values may be sent and summed in bfloat16 or wider, within the bound.
A program may use at most 64 MiB of HBM per device.

```python
import math
import jax
import jax.numpy as jnp

N = 2048
Q = 2048
K = 48
NPTS = 32


def plant(result, rng, least, top_value):
    place = [jax.random.randint(jax.random.fold_in(rng, axis), (), 0, length) for axis, length in enumerate(result.shape)]
    longest = result.shape.index(max(result.shape))
    neighbour = place[:longest] + [(place[longest] + 1) % result.shape[longest]] + place[longest + 1:]
    return result.at[tuple(place)].set(least).at[tuple(neighbour)].set(top_value)


def block_levels(own_key, extent, shards, least, high):
    level = 1.0
    for axis_at, parts in shards:
        steps = jax.random.uniform(jax.random.fold_in(jax.random.fold_in(own_key, 6), axis_at), (parts,), jnp.float32, least / len(shards), high / len(shards))
        level = level * jnp.repeat(jnp.exp(steps), extent[axis_at] // parts).reshape((-1,) + (1,) * (len(extent) - 1 - axis_at))
    return level


def bell_draw(own_key, extent, spread, most, cuts=(), kind=jnp.bfloat16):
    values = jax.random.normal(own_key, extent, jnp.float32) * spread
    if len(cuts) > 0:
        values = block_levels(own_key, extent, cuts, -0.22, 0.18) * values
    return jnp.clip(values, min=-most, max=most).astype(kind)


def setup_inputs(seed: int = 0) -> dict:
    seeds = jax.random.split(jax.random.key(seed), 6)
    return {
        "angular": bell_draw(seeds[0], (Q, N), Q ** -0.5, 0.125, ((1, 32),)),
        "potential": jnp.clip(jnp.exp(jax.random.uniform(seeds[1], (NPTS, Q), jnp.float32, math.log(0.25), math.log(4.0))), 0.25, 4.0),
        "point_rows": jax.random.permutation(seeds[2], NPTS).astype(jnp.int32),
        "quanta": plant(jax.random.randint(seeds[3], (2, N), 0, 8), jax.random.fold_in(seeds[3], 1), 0, 7).astype(jnp.int32),
        "start_waves": bell_draw(seeds[4], (K, N), 1.0, 6.0, ((1, 32),), jnp.float32),
    }


energy = 3.5
rotor_const = 0.02
radius_first = 8.0
radius_step = 0.5
step_square = 0.08

def reference(angular, potential, point_rows, quanta, start_waves):
    j_values = quanta[0].astype(jnp.float32)
    l_values = quanta[1].astype(jnp.float32)
    earlier = jnp.zeros_like(start_waves)
    current = start_waves
    collected = []
    for point_index in range(NPTS):
        radius = radius_first + radius_step * point_index
        root_pot = jnp.sqrt(potential[point_rows[point_index]])
        scaled = (root_pot[:, None] * angular.astype(jnp.float32)).astype(jnp.bfloat16)
        coupling = jnp.dot(scaled.T, scaled, preferred_element_type=jnp.float32).astype(jnp.bfloat16)
        levels = energy - rotor_const * j_values * (j_values + 1.0) - l_values * (l_values + 1.0) / (radius * radius)
        coupled = jnp.dot(current.astype(jnp.bfloat16), coupling, preferred_element_type=jnp.float32)
        following = (2.0 - step_square * levels)[None, :] * current - earlier - step_square * coupled
        earlier = current
        current = following
        collected.append(following)
    return jnp.stack(collected)
```

```python
import functools

import jax
import jax.numpy as jnp
from jax import lax
from jax.experimental import pallas as pl
from jax.experimental.pallas import tpu as pltpu
from jax.sharding import PartitionSpec as P

energy = 3.5
rotor_const = 0.02
radius_first = 8.0
radius_step = 0.5
step_square = 0.08

GROUPS = (5, 5, 6)
TILE = 512
MESH = pl.DeviceIdType.MESH


def pick(index, values):
    result = values[-1]
    for place in range(len(values) - 1):
        result = jnp.where(index == place, values[place], result)
    return result


def kernel(
    chans, sectors,
    full_ref, rows_ref, pot_ref, quanta_ref, start_ref, out_ref,
    basis, flipped, state, rounded, weighted, turned,
    whole, message, terms, table, level_send, level_recv, wave_send, wave_recv, hop_send, hop_recv, load_sem,
):
    n = basis.shape[0]
    width = n // chans
    solutions = start_ref.shape[0]
    sector, me = lax.axis_index("sector"), lax.axis_index("chan")
    group_of, first_of, last_of, next_of = [], [], [], []
    start = 0
    for index, size in enumerate(GROUPS):
        following = GROUPS[index + 1] if index + 1 < len(GROUPS) else 0
        for _ in range(size):
            first_of.append(start)
            last_of.append(start + size - 1)
            next_of.append(following)
        start += size
    first = pick(sector, first_of)
    last = pick(sector, last_of)
    following = pick(sector, next_of)
    sends = jnp.logical_and(sector == last, following > 0)
    previous = first - 1

    load = pltpu.make_async_copy(full_ref, basis, load_sem)
    load.start()

    barrier = pltpu.get_barrier_semaphore()

    def greet(distance, carry):
        peer = lax.rem(me + distance, chans)
        pl.semaphore_signal(barrier, inc=1, device_id=(sector, peer), device_id_type=MESH)
        return carry

    lax.fori_loop(1, chans, greet, 0)

    @pl.when(sends)
    def _():
        def greet_next(step, carry):
            pl.semaphore_signal(barrier, inc=1, device_id=(sector + 1 + step, me), device_id_type=MESH)
            return carry

        lax.fori_loop(0, following, greet_next, 0)

    @pl.when(first > 0)
    def _():
        pl.semaphore_signal(barrier, inc=1, device_id=(previous, me), device_id_type=MESH)

    greeted = chans - 1 + jnp.where(sends, following, 0) + jnp.where(first > 0, 1, 0)
    pl.semaphore_wait(barrier, greeted)

    quanta = quanta_ref[...].astype(jnp.float32)
    j_values, l_values = quanta[0:1, :], quanta[1:2, :]
    a_row = 2.0 - step_square * (energy - rotor_const * j_values * (j_values + 1.0))
    b_row = step_square * (l_values * (l_values + 1.0))
    ab = jnp.concatenate([a_row, b_row, jnp.zeros((6, width), jnp.float32)], axis=0)
    lane = lax.broadcasted_iota(jnp.int32, (8, 2 * width), 1)
    half = lane // width
    terms[me] = jnp.where(half == lax.rem(me, 2), jnp.concatenate([ab, ab], axis=1), 0.0)

    def level_copy(peer):
        return pltpu.make_async_remote_copy(
            src_ref=terms.at[me], dst_ref=terms.at[me],
            send_sem=level_send.at[peer], recv_sem=level_recv.at[me],
            device_id=(sector, peer), device_id_type=MESH,
        )

    def wave_slot(owner):
        return whole.at[:, pl.ds(pl.multiple_of(owner * 2 * width, 2 * width), 2 * width)]

    def wave_copy(peer):
        return pltpu.make_async_remote_copy(
            src_ref=wave_slot(me), dst_ref=wave_slot(me),
            send_sem=wave_send.at[peer], recv_sem=wave_recv.at[me],
            device_id=(sector, peer), device_id_type=MESH,
        )

    def to_peers(make):
        def go(distance, carry):
            make(lax.rem(me + distance, chans)).start()
            return carry

        lax.fori_loop(1, chans, go, 0)

    def sent_to_peers(make):
        def go(distance, carry):
            make(lax.rem(me + distance, chans)).wait_send()
            return carry

        lax.fori_loop(1, chans, go, 0)

    to_peers(level_copy)

    @pl.when(first == 0)
    def _():
        waves = start_ref[...].astype(jnp.bfloat16)
        whole[:, pl.ds(pl.multiple_of(me * 2 * width, 2 * width), 2 * width)] = jnp.concatenate(
            [waves, waves], axis=1
        )
        to_peers(wave_copy)

    load.wait()

    @pl.loop(0, n // 128)
    def _(block):
        rows = pl.ds(pl.multiple_of(block * 128, 128), 128)

        @pl.loop(0, n // TILE)
        def _(tile):
            columns = pl.ds(pl.multiple_of(tile * TILE, TILE), TILE)
            flipped[columns, rows] = jnp.transpose(basis[rows, columns])

    def level_wait(distance, carry):
        owner = lax.rem(me + distance, chans)
        pltpu.make_async_remote_copy(
            src_ref=terms.at[owner], dst_ref=terms.at[owner],
            send_sem=level_send.at[owner], recv_sem=level_recv.at[owner],
            device_id=(sector, owner), device_id_type=MESH,
        ).wait_recv()
        return carry

    lax.fori_loop(1, chans, level_wait, 0)

    @pl.loop(0, chans // 2)
    def _(pair):
        table[:, pl.ds(pl.multiple_of(pair * 128, 128), 128)] = terms[2 * pair] + terms[2 * pair + 1]

    top = 2 * sector + 1
    bottom = 2 * first

    @pl.loop(0, n // TILE)
    def _(tile):
        columns = pl.ds(pl.multiple_of(tile * TILE, TILE), TILE)
        shape = (2 * width, TILE)
        row = lax.broadcasted_iota(jnp.int32, shape, 0)
        column = lax.broadcasted_iota(jnp.int32, shape, 1) + tile * TILE
        later = row < width
        own = column == me * width + jnp.where(later, row, row - width)
        now = jnp.where(jnp.logical_and(own, later), 1.0, 0.0)
        state[0, :, columns] = now
        state[1, :, columns] = jnp.where(jnp.logical_and(own, jnp.logical_not(later)), -1.0, 0.0)
        rounded[:, columns] = now.astype(jnp.bfloat16)

    def back(step, carry):
        point = top - step
        current, other = lax.rem(step, 2), 1 - lax.rem(step, 2)
        row = rows_ref[point]

        @pl.loop(0, n // TILE)
        def _(tile):
            columns = pl.ds(pl.multiple_of(tile * TILE, TILE), TILE)
            product = jnp.dot(rounded[...], basis[:, columns], preferred_element_type=jnp.float32)
            weighted[:, columns] = (product * pot_ref[pl.ds(row, 1), columns]).astype(jnp.bfloat16)

        radius = jnp.full((1, TILE), radius_first, jnp.float32) + radius_step * point.astype(jnp.float32)
        inverse = 1.0 / (radius * radius)

        @pl.loop(0, n // TILE)
        def _(tile):
            columns = pl.ds(pl.multiple_of(tile * TILE, TILE), TILE)
            product = jnp.dot(weighted[...], flipped[:, columns], preferred_element_type=jnp.float32)
            factor = table[0:1, columns] + table[1:2, columns] * inverse
            new = factor * state[current, :, columns] - state[other, :, columns] - step_square * product
            state[other, :, columns] = new
            rounded[:, columns] = new.astype(jnp.bfloat16)

        return carry

    steps = top - bottom + 1
    lax.fori_loop(0, steps, back, 0)
    newest, older = lax.rem(steps, 2), 1 - lax.rem(steps, 2)

    low = lax.broadcasted_iota(jnp.int32, (2 * width, 128), 1) < width

    def differences(rows):
        return jnp.concatenate([rows[:width], rows[:width] - rows[width:]], axis=0)

    @pl.loop(0, chans // 2)
    def _(pair):
        columns = pl.ds(pl.multiple_of(pair * 128, 128), 128)
        before = differences(state[older, :, columns])
        main = differences(state[newest, :, columns]) - before
        left = jnp.where(low, main, pltpu.roll(before, width, 1))
        right = jnp.where(low, pltpu.roll(main, width, 1), before)
        turned[pl.ds(pl.multiple_of(pair * 256, 256), 128), :] = jnp.transpose(left).astype(jnp.bfloat16)
        turned[pl.ds(pl.multiple_of(pair * 256 + 128, 128), 128), :] = jnp.transpose(right).astype(jnp.bfloat16)

    @pl.when(first > 0)
    def _():
        pltpu.make_async_remote_copy(
            src_ref=message, dst_ref=wave_slot(me), send_sem=hop_send.at[0], recv_sem=hop_recv,
            device_id=(previous, me), device_id_type=MESH,
        ).wait_recv()
        to_peers(wave_copy)

    def wave_wait(distance, carry):
        owner = lax.rem(me + distance, chans)
        pltpu.make_async_remote_copy(
            src_ref=wave_slot(owner), dst_ref=wave_slot(owner),
            send_sem=wave_send.at[owner], recv_sem=wave_recv.at[owner],
            device_id=(sector, owner), device_id_type=MESH,
        ).wait_recv()
        return carry

    lax.fori_loop(1, chans, wave_wait, 0)
    result = jnp.dot(whole[...], turned[...], preferred_element_type=jnp.float32)
    swapped = pltpu.roll(result, width, 1)

    def hop_copy(step):
        return pltpu.make_async_remote_copy(
            src_ref=message, dst_ref=wave_slot(me), send_sem=hop_send.at[step], recv_sem=hop_recv,
            device_id=(sector + 1 + step, me), device_id_type=MESH,
        )

    @pl.when(sends)
    def _():
        message[...] = result.astype(jnp.bfloat16)

        def go(step, carry):
            hop_copy(following - 1 - step).start()
            return carry

        lax.fori_loop(0, following, go, 0)

        def done(step, carry):
            hop_copy(step).wait_send()
            return carry

        lax.fori_loop(0, following, done, 0)

    out_ref[0] = (result - swapped)[:, :width]
    out_ref[1] = result[:, :width]
    sent_to_peers(level_copy)
    sent_to_peers(wave_copy)


def local(angular, potential, point_rows, quanta, start_waves):
    chans, sectors = lax.axis_size("chan"), lax.axis_size("sector")
    points, n = angular.shape[0], angular.shape[1] * chans
    solutions, width = start_waves.shape
    full = lax.all_gather(angular.T, "chan", axis=0, tiled=True)
    vmem = pl.BlockSpec(memory_space=pltpu.VMEM)
    return pl.pallas_call(
        functools.partial(kernel, chans, sectors),
        out_shape=jax.ShapeDtypeStruct((2, solutions, width), jnp.float32),
        in_specs=[
            pl.BlockSpec(memory_space=pl.ANY),
            pl.BlockSpec(memory_space=pltpu.SMEM),
            vmem, vmem, vmem,
        ],
        out_specs=vmem,
        scratch_shapes=[
            pltpu.VMEM((n, points), jnp.bfloat16),
            pltpu.VMEM((points, n), jnp.bfloat16),
            pltpu.VMEM((2, 2 * width, n), jnp.float32),
            pltpu.VMEM((2 * width, n), jnp.bfloat16),
            pltpu.VMEM((2 * width, points), jnp.bfloat16),
            pltpu.VMEM((2 * n, 2 * width), jnp.bfloat16),
            pltpu.VMEM((solutions, 2 * n), jnp.bfloat16),
            pltpu.VMEM((solutions, 2 * width), jnp.bfloat16),
            pltpu.VMEM((chans, 8, 2 * width), jnp.float32),
            pltpu.VMEM((8, n), jnp.float32),
            pltpu.SemaphoreType.DMA((chans,)),
            pltpu.SemaphoreType.DMA((chans,)),
            pltpu.SemaphoreType.DMA((chans,)),
            pltpu.SemaphoreType.DMA((chans,)),
            pltpu.SemaphoreType.DMA((max(GROUPS),)),
            pltpu.SemaphoreType.DMA,
            pltpu.SemaphoreType.DMA,
        ],
        compiler_params=pltpu.CompilerParams(
            collective_id=0, has_side_effects=True, vmem_limit_bytes=48 * 1024 * 1024
        ),
    )(full, point_rows, potential, quanta, start_waves)


def solution(mesh):
    placed = (P(None, "chan"), P(), P(), P(None, "chan"), P(None, "chan"))
    return jax.shard_map(
        local, mesh=mesh, in_specs=placed, out_specs=P("sector", None, "chan"), check_vma=False
    )
```

```python
import functools

import jax
import jax.numpy as jnp
from jax import lax
from jax.experimental import pallas as pl
from jax.experimental.pallas import tpu as pltpu
from jax.sharding import PartitionSpec as P

energy = 3.5
rotor_const = 0.02
radius_first = 8.0
radius_step = 0.5
step_square = 0.08

GROUPS = (5, 5, 6)
TILE = 512
MESH = pl.DeviceIdType.MESH

SIDE = 4
ACROSS = (0, -1, 1)
PIECES = (
    [(-1, 0, None), (1, 0, None), (2, 0, 0), (2, 0, 1)]
    + [(step, -1, None) for step in ACROSS] + [(2, -1, 0), (2, -1, 1)]
    + [(step, 1, None) for step in ACROSS] + [(2, 1, 0), (2, 1, 1)]
    + [(step, 2, 0) for step in ACROSS + (2,)] + [(step, 2, 1) for step in ACROSS + (2,)]
)
OWN = len(PIECES)
FORE, BACK, UP, DOWN = (1, 0), (-1, 0), (0, 1), (0, -1)
OWN_TO = [(FORE, 0), (BACK, 1), (UP, 4), (DOWN, 9)]
FORWARD = [
    [(0, FORE, 2), (None, UP, 5), (None, DOWN, 10)],
    [(1, BACK, 3), (None, UP, 6), (None, DOWN, 11)],
    [(None, UP, 7), (None, DOWN, 12)],
    [(None, UP, 8), (None, DOWN, 13)],
    [(0, UP, 14)], [(0, UP, 15)], [(0, UP, 16)], [(None, UP, 17)], [],
    [(1, DOWN, 18)], [(1, DOWN, 19)], [(1, DOWN, 20)], [], [(None, DOWN, 21)],
] + [[]] * 8
STAGES = [
    ([0, 1, 4, 9], [(0, 0)]),
    ([2, 3, 5, 10, 6, 11], [(-1, 0), (1, 0), (0, -1), (0, 1)]),
    ([7, 12, 8, 13, 14, 18], [(-1, -1), (-1, 1), (1, -1), (1, 1), (2, 0), (0, 2)]),
    ([15, 19, 16, 20, 17, 21], [(2, -1), (2, 1), (-1, 2), (1, 2), (2, 2)]),
]


def pick(index, values):
    result = values[-1]
    for place in range(len(values) - 1):
        result = jnp.where(index == place, values[place], result)
    return result


def kernel(
    chans, sectors,
    mine_ref, rows_ref, pot_ref, quanta_ref, start_ref, out_ref,
    basis, flipped, state, rounded, weighted, summed, turned,
    whole, message, terms, table, level_send, level_recv, wave_send, wave_recv, hop_send, hop_recv,
    ring_send, ring_recv, twin_send, twin_recv,
):
    n = basis.shape[0]
    width = n // chans
    solutions = start_ref.shape[0]
    sector, me = lax.axis_index("sector"), lax.axis_index("chan")
    group_of, first_of, last_of, next_of = [], [], [], []
    start = 0
    for index, size in enumerate(GROUPS):
        following = GROUPS[index + 1] if index + 1 < len(GROUPS) else 0
        for _ in range(size):
            first_of.append(start)
            last_of.append(start + size - 1)
            next_of.append(following)
        start += size
    first = pick(sector, first_of)
    last = pick(sector, last_of)
    following = pick(sector, next_of)
    sends = jnp.logical_and(sector == last, following > 0)
    previous = first - 1

    barrier = pltpu.get_barrier_semaphore()

    def greet(distance, carry):
        peer = lax.rem(me + distance, chans)
        pl.semaphore_signal(barrier, inc=1, device_id=(sector, peer), device_id_type=MESH)
        return carry

    lax.fori_loop(1, chans, greet, 0)

    @pl.when(sends)
    def _():
        def greet_next(step, carry):
            pl.semaphore_signal(barrier, inc=1, device_id=(sector + 1 + step, me), device_id_type=MESH)
            return carry

        lax.fori_loop(0, following, greet_next, 0)

    @pl.when(first > 0)
    def _():
        pl.semaphore_signal(barrier, inc=1, device_id=(previous, me), device_id_type=MESH)

    greeted = chans - 1 + jnp.where(sends, following, 0) + jnp.where(first > 0, 1, 0)
    pl.semaphore_wait(barrier, greeted)

    quanta = quanta_ref[...].astype(jnp.float32)
    j_values, l_values = quanta[0:1, :], quanta[1:2, :]
    a_row = 2.0 - step_square * (energy - rotor_const * j_values * (j_values + 1.0))
    b_row = step_square * (l_values * (l_values + 1.0))
    ab = jnp.concatenate([a_row, b_row, jnp.zeros((6, width), jnp.float32)], axis=0)
    lane = lax.broadcasted_iota(jnp.int32, (8, 2 * width), 1)
    half = lane // width
    terms[me] = jnp.where(half == lax.rem(me, 2), jnp.concatenate([ab, ab], axis=1), 0.0)

    def level_copy(peer):
        return pltpu.make_async_remote_copy(
            src_ref=terms.at[me], dst_ref=terms.at[me],
            send_sem=level_send.at[peer], recv_sem=level_recv.at[me],
            device_id=(sector, peer), device_id_type=MESH,
        )

    def wave_slot(owner):
        return whole.at[:, pl.ds(pl.multiple_of(owner * 2 * width, 2 * width), 2 * width)]

    def wave_copy(peer):
        return pltpu.make_async_remote_copy(
            src_ref=wave_slot(me), dst_ref=wave_slot(me),
            send_sem=wave_send.at[peer], recv_sem=wave_recv.at[me],
            device_id=(sector, peer), device_id_type=MESH,
        )

    def to_peers(make):
        def go(distance, carry):
            make(lax.rem(me + distance, chans)).start()
            return carry

        lax.fori_loop(1, chans, go, 0)

    def sent_to_peers(make):
        def go(distance, carry):
            make(lax.rem(me + distance, chans)).wait_send()
            return carry

        lax.fori_loop(1, chans, go, 0)

    core, y_at, x_at = lax.rem(me, 2), lax.rem(me // 2, SIDE), me // (2 * SIDE)
    twin = me + 1 - 2 * core
    cut = n // 2

    def chip_of(half, first_step, second_step):
        dx, dy = (first_step, second_step) if half == 0 else (second_step, first_step)
        return lax.rem(x_at + dx + SIDE, SIDE) * SIDE + lax.rem(y_at + dy + SIDE, SIDE)

    def piece(half, owner, part):
        begin, size = (0, width) if part is None else (part * (width // 2), width // 2)
        rows = pl.ds(pl.multiple_of(owner * width + begin, width // 2), size)
        return basis.at[rows, pl.ds(half * cut, cut)]

    def ring_copy(half, first_step, second_step, part, toward, slot, source=None):
        owner = chip_of(half, first_step, second_step) * 2 + core
        return pltpu.make_async_remote_copy(
            src_ref=piece(half, owner, part) if source is None else source,
            dst_ref=piece(half, owner, part),
            send_sem=ring_send.at[half, slot], recv_sem=ring_recv.at[half, slot],
            device_id=(sector, chip_of(half, *toward) * 2 + core), device_id_type=MESH,
        )

    def twin_copy(half, slot, owner):
        part = PIECES[slot][2]
        return pltpu.make_async_remote_copy(
            src_ref=piece(half, owner, part), dst_ref=piece(half, owner, part),
            send_sem=twin_send.at[half, slot], recv_sem=twin_recv.at[half, slot],
            device_id=(sector, twin), device_id_type=MESH,
        )

    def arrived(half, slot):
        first_step, second_step, part = PIECES[slot]
        ring_copy(half, first_step, second_step, part, (0, 1), slot).wait_recv()
        for cut_to, toward, target in FORWARD[slot]:
            ring_copy(half, first_step, second_step, part if cut_to is None else cut_to, toward, target).start()
        twin_copy(half, slot, chip_of(half, first_step, second_step) * 2 + core).start()

    def twin_arrived(half, slot):
        first_step, second_step, _ = PIECES[slot]
        twin_copy(half, slot, chip_of(half, first_step, second_step) * 2 + 1 - core).wait_recv()

    def own_twin_copy(owner):
        place = basis.at[pl.ds(pl.multiple_of(owner * width, width), width), :]
        return pltpu.make_async_remote_copy(
            src_ref=mine_ref, dst_ref=place, send_sem=twin_send.at[0, OWN], recv_sem=twin_recv.at[0, OWN],
            device_id=(sector, twin), device_id_type=MESH,
        )

    for half in (0, 1):
        for toward, target in OWN_TO:
            ring_copy(
                half, 0, 0, None, toward, target, mine_ref.at[:, pl.ds(half * cut, cut)]
            ).start()
    own_twin_copy(me).start()
    basis[pl.ds(pl.multiple_of(me * width, width), width), :] = mine_ref[...]

    to_peers(level_copy)

    @pl.when(first == 0)
    def _():
        waves = start_ref[...].astype(jnp.bfloat16)
        whole[:, pl.ds(pl.multiple_of(me * 2 * width, 2 * width), 2 * width)] = jnp.concatenate(
            [waves, waves], axis=1
        )
        to_peers(wave_copy)

    top = 2 * sector + 1
    bottom = 2 * first
    top_row = rows_ref[top]
    weighted[pl.ds(0, width), :] = (
        mine_ref[...].astype(jnp.float32) * pot_ref[pl.ds(top_row, 1), :]
    ).astype(jnp.bfloat16)
    summed[...] = jnp.zeros_like(summed)

    def factor_of(point, columns, size):
        radius = jnp.full((1, size), radius_first, jnp.float32) + radius_step * point.astype(jnp.float32)
        return table[0:1, columns] + table[1:2, columns] * (1.0 / (radius * radius))

    def take(chip):
        columns = pl.ds(pl.multiple_of(chip * 128, 128), 128)
        for begin in range(0, n, TILE):
            flipped[pl.ds(begin, TILE), columns] = jnp.transpose(basis[columns, pl.ds(begin, TILE)])
        product = jnp.dot(weighted[pl.ds(0, width), :], flipped[:, columns], preferred_element_type=jnp.float32)
        row = lax.broadcasted_iota(jnp.int32, (width, 128), 0)
        column = lax.broadcasted_iota(jnp.int32, (width, 128), 1) + chip * 128
        own = jnp.where(column == me * width + row, 1.0, 0.0)
        new = factor_of(top, columns, 128) * own - step_square * product
        both = jnp.concatenate([new, own], axis=0)
        state[0, :, columns] = jnp.concatenate([own, jnp.zeros_like(own)], axis=0)
        state[1, :, columns] = both
        both = both.astype(jnp.bfloat16)
        for begin in range(0, n, TILE):
            tile = pl.ds(begin, TILE)
            summed[:, tile] += jnp.dot(both, basis[columns, tile], preferred_element_type=jnp.float32)

    def level_wait(distance, carry):
        owner = lax.rem(me + distance, chans)
        pltpu.make_async_remote_copy(
            src_ref=terms.at[owner], dst_ref=terms.at[owner],
            send_sem=level_send.at[owner], recv_sem=level_recv.at[owner],
            device_id=(sector, owner), device_id_type=MESH,
        ).wait_recv()
        return carry

    for stage, (slots, offsets) in enumerate(STAGES):
        for slot in slots:
            for half in (0, 1):
                arrived(half, slot)
        if stage == 0:
            lax.fori_loop(1, chans, level_wait, 0)

            @pl.loop(0, chans // 2)
            def _(pair):
                table[:, pl.ds(pl.multiple_of(pair * 128, 128), 128)] = terms[2 * pair] + terms[2 * pair + 1]

            own_twin_copy(twin).wait_recv()
        for slot in slots:
            for half in (0, 1):
                twin_arrived(half, slot)

        def each(index, carry, offsets=offsets):
            dx, dy = pick(index, [o[0] for o in offsets]), pick(index, [o[1] for o in offsets])
            take(chip_of(0, dx, dy))
            return carry

        lax.fori_loop(0, len(offsets), each, 0)

    steps = top - bottom + 1

    def weigh(product, point, columns):
        weighted[:, columns] = (product * pot_ref[pl.ds(rows_ref[point], 1), columns]).astype(jnp.bfloat16)

    for begin in range(0, n, TILE):
        weigh(summed[:, pl.ds(begin, TILE)], top - 1, pl.ds(begin, TILE))

    def back(step, carry):
        point = top - step
        current, other = lax.rem(step, 2), 1 - lax.rem(step, 2)
        for begin in range(0, n, TILE):
            columns = pl.ds(begin, TILE)
            product = jnp.dot(weighted[...], flipped[:, columns], preferred_element_type=jnp.float32)
            new = (
                factor_of(point, columns, TILE) * state[current, :, columns]
                - state[other, :, columns] - step_square * product
            )
            state[other, :, columns] = new
            rounded[:, columns] = new.astype(jnp.bfloat16)

        @pl.when(step + 1 < steps)
        def _():
            for begin in range(0, n, TILE):
                columns = pl.ds(begin, TILE)
                weigh(
                    jnp.dot(rounded[...], basis[:, columns], preferred_element_type=jnp.float32),
                    point - 1, columns,
                )

        return carry

    lax.fori_loop(1, steps, back, 0)
    newest, older = lax.rem(steps, 2), 1 - lax.rem(steps, 2)

    low = lax.broadcasted_iota(jnp.int32, (2 * width, 128), 1) < width

    def differences(rows):
        return jnp.concatenate([rows[:width], rows[:width] - rows[width:]], axis=0)

    @pl.loop(0, chans // 2)
    def _(pair):
        columns = pl.ds(pl.multiple_of(pair * 128, 128), 128)
        before = differences(state[older, :, columns])
        main = differences(state[newest, :, columns]) - before
        left = jnp.where(low, main, pltpu.roll(before, width, 1))
        right = jnp.where(low, pltpu.roll(main, width, 1), before)
        turned[pl.ds(pl.multiple_of(pair * 256, 256), 128), :] = jnp.transpose(left).astype(jnp.bfloat16)
        turned[pl.ds(pl.multiple_of(pair * 256 + 128, 128), 128), :] = jnp.transpose(right).astype(jnp.bfloat16)

    @pl.when(first > 0)
    def _():
        pltpu.make_async_remote_copy(
            src_ref=message, dst_ref=wave_slot(me), send_sem=hop_send.at[0], recv_sem=hop_recv,
            device_id=(previous, me), device_id_type=MESH,
        ).wait_recv()
        to_peers(wave_copy)

    def wave_wait(distance, carry):
        owner = lax.rem(me + distance, chans)
        pltpu.make_async_remote_copy(
            src_ref=wave_slot(owner), dst_ref=wave_slot(owner),
            send_sem=wave_send.at[owner], recv_sem=wave_recv.at[owner],
            device_id=(sector, owner), device_id_type=MESH,
        ).wait_recv()
        return carry

    lax.fori_loop(1, chans, wave_wait, 0)
    result = jnp.dot(whole[...], turned[...], preferred_element_type=jnp.float32)
    swapped = pltpu.roll(result, width, 1)

    def hop_copy(step):
        return pltpu.make_async_remote_copy(
            src_ref=message, dst_ref=wave_slot(me), send_sem=hop_send.at[step], recv_sem=hop_recv,
            device_id=(sector + 1 + step, me), device_id_type=MESH,
        )

    @pl.when(sends)
    def _():
        message[...] = result.astype(jnp.bfloat16)

        def go(step, carry):
            hop_copy(following - 1 - step).start()
            return carry

        lax.fori_loop(0, following, go, 0)

        def done(step, carry):
            hop_copy(step).wait_send()
            return carry

        lax.fori_loop(0, following, done, 0)

    out_ref[0] = (result - swapped)[:, :width]
    out_ref[1] = result[:, :width]
    sent_to_peers(level_copy)
    sent_to_peers(wave_copy)
    for half in (0, 1):
        for toward, target in OWN_TO:
            ring_copy(half, 0, 0, None, toward, target).wait_send()
        for slot, (first_step, second_step, part) in enumerate(PIECES):
            for cut_to, toward, target in FORWARD[slot]:
                ring_copy(half, first_step, second_step, part if cut_to is None else cut_to, toward, target).wait_send()
            twin_copy(half, slot, me).wait_send()
    own_twin_copy(me).wait_send()


def local(angular, potential, point_rows, quanta, start_waves):
    chans, sectors = lax.axis_size("chan"), lax.axis_size("sector")
    points, n = angular.shape[0], angular.shape[1] * chans
    solutions, width = start_waves.shape
    vmem = pl.BlockSpec(memory_space=pltpu.VMEM)
    return pl.pallas_call(
        functools.partial(kernel, chans, sectors),
        out_shape=jax.ShapeDtypeStruct((2, solutions, width), jnp.float32),
        in_specs=[
            vmem,
            pl.BlockSpec(memory_space=pltpu.SMEM),
            vmem, vmem, vmem,
        ],
        out_specs=vmem,
        scratch_shapes=[
            pltpu.VMEM((n, points), jnp.bfloat16),
            pltpu.VMEM((points, n), jnp.bfloat16),
            pltpu.VMEM((2, 2 * width, n), jnp.float32),
            pltpu.VMEM((2 * width, n), jnp.bfloat16),
            pltpu.VMEM((2 * width, points), jnp.bfloat16),
            pltpu.VMEM((2 * width, points), jnp.float32),
            pltpu.VMEM((2 * n, 2 * width), jnp.bfloat16),
            pltpu.VMEM((solutions, 2 * n), jnp.bfloat16),
            pltpu.VMEM((solutions, 2 * width), jnp.bfloat16),
            pltpu.VMEM((chans, 8, 2 * width), jnp.float32),
            pltpu.VMEM((8, n), jnp.float32),
            pltpu.SemaphoreType.DMA((chans,)),
            pltpu.SemaphoreType.DMA((chans,)),
            pltpu.SemaphoreType.DMA((chans,)),
            pltpu.SemaphoreType.DMA((chans,)),
            pltpu.SemaphoreType.DMA((max(GROUPS),)),
            pltpu.SemaphoreType.DMA,
            pltpu.SemaphoreType.DMA((2, OWN)),
            pltpu.SemaphoreType.DMA((2, OWN)),
            pltpu.SemaphoreType.DMA((2, OWN + 1)),
            pltpu.SemaphoreType.DMA((2, OWN + 1)),
        ],
        compiler_params=pltpu.CompilerParams(
            collective_id=0, has_side_effects=True, vmem_limit_bytes=48 * 1024 * 1024
        ),
    )(angular.T, point_rows, potential, quanta, start_waves)


def solution(mesh):
    placed = (P(None, "chan"), P(), P(), P(None, "chan"), P(None, "chan"))
    return jax.shard_map(
        local, mesh=mesh, in_specs=placed, out_specs=P("sector", None, "chan"), check_vma=False
    )
```

```python
import functools

import jax
import jax.numpy as jnp
from jax import lax
from jax.experimental import pallas as pl
from jax.experimental.pallas import tpu as pltpu
from jax.sharding import PartitionSpec as P

energy = 3.5
rotor_const = 0.02
radius_first = 8.0
radius_step = 0.5
step_square = 0.08

GROUPS = (3, 5, 8)
PASS_AT = (99, 8, 12)
TILE = 512
MESH = pl.DeviceIdType.MESH

SIDE = 4
STEPS = (0, -1, 1, 2)
PIECES = [(f, s, part) for f in STEPS for s in STEPS if (f, s) != (0, 0) for part in (0, 1)]
OWN = len(PIECES)
FORE, BACK, UP, DOWN = (1, 0), (-1, 0), (0, 1), (0, -1)
OWN_TO = [
    (part, toward, PIECES.index((-toward[0], -toward[1], part)))
    for turn in (0, 1)
    for toward, early in ((FORE, 0), (BACK, 1), (UP, 0), (DOWN, 1))
    for part in (early if turn == 0 else 1 - early,)
]


def sent_on(piece):
    f, s, part = piece
    result = []
    if s == 0:
        if (f, part) == (-1, 0):
            result.append((FORE, PIECES.index((2, 0, 0))))
        if (f, part) == (1, 1):
            result.append((BACK, PIECES.index((2, 0, 1))))
        result += [(UP, PIECES.index((f, -1, part))), (DOWN, PIECES.index((f, 1, part)))]
    if (s, part) == (-1, 0):
        result.append((UP, PIECES.index((f, 2, 0))))
    if (s, part) == (1, 1):
        result.append((DOWN, PIECES.index((f, 2, 1))))
    return result


FORWARD = [sent_on(piece) for piece in PIECES]
FAR_FIRST = sorted(
    [(dx, dy) for dx in STEPS for dy in STEPS if (dx, dy) != (0, 0)], key=lambda o: -abs(o[0]) - abs(o[1])
)
ORDER = [
    ("pieces", [(-1, 0, 0), (1, 0, 1), (0, -1, 0), (0, 1, 1), (-1, 0, 1), (1, 0, 0), (0, -1, 1), (0, 1, 0)]),
    ("levels", 0), ("take", [(0, 0)]),
    ("pieces", [(2, 0, 0), (2, 0, 1), (-1, -1, 0), (1, -1, 0), (-1, 1, 1), (1, 1, 1)]),
    ("levels", 1), ("take", [(-1, 0), (0, -1)]),
    ("pieces", [(0, 2, 0), (0, 2, 1), (-1, -1, 1), (1, -1, 1), (-1, 1, 0), (1, 1, 0)]),
    ("take", [(1, 0), (0, 1)]),
    ("pieces", [(2, -1, 0), (2, 1, 1)]), ("take", [(-1, -1), (1, -1)]),
    ("pieces", [(2, -1, 1), (2, 1, 0)]), ("take", [(-1, 1), (1, 1)]),
    ("pieces", [(-1, 2, 0), (-1, 2, 1)]), ("take", [(2, 0), (0, 2)]),
    ("pieces", [(1, 2, 0), (1, 2, 1)]), ("take", [(2, -1), (-1, 2)]),
    ("waves", 0), ("waves", 1), ("take", [(2, 1), (1, 2)]), ("pieces", [(2, 2, 0), (2, 2, 1)]), ("take", [(2, 2)]),
]


def pick(index, values):
    result = values[-1]
    for place in range(len(values) - 1):
        result = jnp.where(index == place, values[place], result)
    return result


def kernel(
    chans, sectors,
    mine_ref, rows_ref, pot_in, quanta_in, start_in, out_ref,
    pot_ref, quanta_ref, start_ref,
    basis, flipped, state, rounded, weighted, summed, turned,
    whole, message, terms, table, level_send, level_recv, wave_send, wave_recv, hop_send, hop_recv,
    ring_send, ring_recv, twin_send, twin_recv, load_sem,
):
    n = basis.shape[0]
    width = n // chans
    sector, me = lax.axis_index("sector"), lax.axis_index("chan")
    first_of, last_of, next_of, pass_of = [], [], [], []
    start = 0
    for index, size in enumerate(GROUPS):
        following = GROUPS[index + 1] if index + 1 < len(GROUPS) else 0
        for _ in range(size):
            first_of.append(start)
            last_of.append(start + size - 1)
            next_of.append(following)
            pass_of.append(PASS_AT[index])
        start += size
    first = pick(sector, first_of)
    last = pick(sector, last_of)
    following = pick(sector, next_of)
    pass_at = pick(sector, pass_of)
    sends = jnp.logical_and(sector == last, following > 0)
    previous = first - 1

    core, y_at, x_at = lax.rem(me, 2), lax.rem(me // 2, SIDE), me // (2 * SIDE)
    twin = me + 1 - 2 * core
    cut = n // 2
    own_rows = pl.ds(pl.multiple_of(me * width, width), width)
    loads = [
        pltpu.make_async_copy(source, place, load_sem.at[index])
        for index, (source, place) in enumerate([
            (quanta_in, quanta_ref), (start_in, start_ref), (mine_ref, basis.at[own_rows, :]), (pot_in, pot_ref),
        ])
    ]
    for load in loads:
        load.start()

    barrier = pltpu.get_barrier_semaphore()

    def greet(distance, carry):
        peer = lax.rem(me + distance, chans)
        pl.semaphore_signal(barrier, inc=1, device_id=(sector, peer), device_id_type=MESH)
        return carry

    lax.fori_loop(1, chans, greet, 0)

    @pl.when(sends)
    def _():
        def greet_next(step, carry):
            pl.semaphore_signal(barrier, inc=1, device_id=(sector + 1 + step, me), device_id_type=MESH)
            return carry

        lax.fori_loop(0, following, greet_next, 0)

    @pl.when(first > 0)
    def _():
        pl.semaphore_signal(barrier, inc=1, device_id=(previous, me), device_id_type=MESH)

    greeted = chans - 1 + jnp.where(sends, following, 0) + jnp.where(first > 0, 1, 0)
    pl.semaphore_wait(barrier, greeted)

    def level_copy(peer):
        return pltpu.make_async_remote_copy(
            src_ref=terms.at[me], dst_ref=terms.at[me],
            send_sem=level_send.at[peer], recv_sem=level_recv.at[me],
            device_id=(sector, peer), device_id_type=MESH,
        )

    def wave_slot(owner):
        return whole.at[:, pl.ds(pl.multiple_of(owner * 2 * width, 2 * width), 2 * width)]

    def wave_copy(peer):
        return pltpu.make_async_remote_copy(
            src_ref=wave_slot(me), dst_ref=wave_slot(me),
            send_sem=wave_send.at[peer], recv_sem=wave_recv.at[me],
            device_id=(sector, peer), device_id_type=MESH,
        )

    def to_peers(make, portion=None):
        for place, (dx, dy) in enumerate(FAR_FIRST):
            if portion in (None, place % 2):
                for side in (0, 1):
                    make(chip_of(0, dx, dy) * 2 + side).start()
        if portion != 0:
            make(twin).start()

    def sent_to_peers(make):
        def go(distance, carry):
            make(lax.rem(me + distance, chans)).wait_send()
            return carry

        lax.fori_loop(1, chans, go, 0)

    def chip_of(half, first_step, second_step):
        dx, dy = (first_step, second_step) if half == 0 else (second_step, first_step)
        return lax.rem(x_at + dx + SIDE, SIDE) * SIDE + lax.rem(y_at + dy + SIDE, SIDE)

    def piece(half, owner, part):
        begin, size = (0, width) if part is None else (part * (width // 2), width // 2)
        rows = pl.ds(pl.multiple_of(owner * width + begin, width // 2), size)
        return basis.at[rows, pl.ds(half * cut, cut)]

    def ring_copy(half, slot, toward, target, source=None):
        first_step, second_step, part = (0, 0, PIECES[target][2]) if slot is None else PIECES[slot]
        owner = chip_of(half, first_step, second_step) * 2 + core
        return pltpu.make_async_remote_copy(
            src_ref=piece(half, owner, part) if source is None else source,
            dst_ref=piece(half, owner, part),
            send_sem=ring_send.at[half, target], recv_sem=ring_recv.at[half, target],
            device_id=(sector, chip_of(half, *toward) * 2 + core), device_id_type=MESH,
        )

    def twin_copy(half, slot, side):
        first_step, second_step, _ = PIECES[slot]
        place = piece(half, chip_of(half, first_step, second_step) * 2 + side, None)
        return pltpu.make_async_remote_copy(
            src_ref=place, dst_ref=place,
            send_sem=twin_send.at[half, slot // 2], recv_sem=twin_recv.at[half, slot // 2],
            device_id=(sector, twin), device_id_type=MESH,
        )

    def arrived(half, slot, both):
        pltpu.make_async_remote_copy(
            src_ref=mine_ref.at[pl.ds(0, width // 2), pl.ds(0, cut)], dst_ref=piece(
                half, chip_of(half, *PIECES[slot][:2]) * 2 + core, PIECES[slot][2]
            ),
            send_sem=ring_send.at[half, slot], recv_sem=ring_recv.at[half, slot],
            device_id=(sector, twin), device_id_type=MESH,
        ).wait_recv()
        for toward, target in FORWARD[slot]:
            ring_copy(half, slot, toward, target).start()
        if both:
            twin_copy(half, slot, core).start()

    def own_twin_copy(owner):
        place = basis.at[pl.ds(pl.multiple_of(owner * width, width), width), :]
        return pltpu.make_async_remote_copy(
            src_ref=mine_ref, dst_ref=place, send_sem=twin_send.at[0, OWN // 2], recv_sem=twin_recv.at[0, OWN // 2],
            device_id=(sector, twin), device_id_type=MESH,
        )

    def own_part(half, part):
        return mine_ref.at[pl.ds(part * (width // 2), width // 2), pl.ds(half * cut, cut)]

    for part, toward, target in OWN_TO:
        for half in (0, 1):
            ring_copy(half, None, toward, target, own_part(half, part)).start()
    own_twin_copy(me).start()

    loads[0].wait()
    quanta = quanta_ref[...].astype(jnp.float32)
    j_values, l_values = quanta[0:1, :], quanta[1:2, :]
    a_row = 2.0 - step_square * (energy - rotor_const * j_values * (j_values + 1.0))
    b_row = step_square * (l_values * (l_values + 1.0))
    ab = jnp.concatenate([a_row, b_row, jnp.zeros((6, width), jnp.float32)], axis=0)
    lane = lax.broadcasted_iota(jnp.int32, (8, 2 * width), 1)
    half = lane // width
    terms[me] = jnp.where(half == lax.rem(me, 2), jnp.concatenate([ab, ab], axis=1), 0.0)
    loads[1].wait()

    @pl.when(first == 0)
    def _():
        waves = start_ref[...].astype(jnp.bfloat16)
        whole[:, pl.ds(pl.multiple_of(me * 2 * width, 2 * width), 2 * width)] = jnp.concatenate(
            [waves, waves], axis=1
        )

    top = 2 * sector + 1
    bottom = 2 * first
    top_row = rows_ref[top]
    loads[2].wait()
    loads[3].wait()
    weighted[pl.ds(0, width), :] = (
        basis[own_rows, :].astype(jnp.float32) * pot_ref[pl.ds(top_row, 1), :]
    ).astype(jnp.bfloat16)
    summed[...] = jnp.zeros_like(summed)

    def level_of(point, a_row, b_row):
        radius = jnp.full(a_row.shape, radius_first, jnp.float32) + radius_step * point.astype(jnp.float32)
        return a_row + b_row * (1.0 / (radius * radius))

    own_level = level_of(top, terms[me, 0:1, :], terms[me, 1:2, :])

    def take(chips):
        places, news = [], []
        for chip in chips:
            columns = pl.ds(pl.multiple_of(chip * 128, 128), 128)
            for begin in range(0, n, TILE):
                flipped[pl.ds(begin, TILE), columns] = jnp.transpose(basis[columns, pl.ds(begin, TILE)])
            places.append(columns)
        for chip, columns in zip(chips, places):
            product = jnp.dot(
                weighted[pl.ds(0, width), :], flipped[:, columns], preferred_element_type=jnp.float32
            )
            row = lax.broadcasted_iota(jnp.int32, (width, 128), 0)
            column = lax.broadcasted_iota(jnp.int32, (width, 128), 1) + chip * 128
            own = jnp.where(column == me * width + row, 1.0, 0.0)
            both = jnp.concatenate([own_level * own - step_square * product, own], axis=0)
            state[0, :, columns] = jnp.concatenate([own, jnp.zeros_like(own)], axis=0)
            state[1, :, columns] = both
            news.append(both.astype(jnp.bfloat16))
        for begin in range(0, n, TILE):
            tile = pl.ds(begin, TILE)
            total = summed[:, tile]
            for columns, both in zip(places, news):
                total += jnp.dot(both, basis[columns, tile], preferred_element_type=jnp.float32)
            summed[:, tile] = total

    def level_wait(distance, carry):
        owner = lax.rem(me + distance, chans)
        pltpu.make_async_remote_copy(
            src_ref=terms.at[owner], dst_ref=terms.at[owner],
            send_sem=level_send.at[owner], recv_sem=level_recv.at[owner],
            device_id=(sector, owner), device_id_type=MESH,
        ).wait_recv()
        return carry

    handed = ([], [])
    for kind, what in ORDER:
        if kind == "pieces":
            for name in what:
                for half in (0, 1):
                    handed[half].append(name)
                    arrived(half, PIECES.index(name), name[:2] + (1 - name[2],) in handed[half])
        elif kind == "levels":
            to_peers(level_copy, what)
        elif kind == "waves":
            @pl.when(first == 0)
            def _(portion=what):
                to_peers(wave_copy, portion)
        else:
            for dx, dy in what:
                if (dx, dy) == (0, 0):
                    own_twin_copy(twin).wait_recv()
                else:
                    for half, steps_to in ((0, (dx, dy)), (1, (dy, dx))):
                        twin_copy(half, PIECES.index(steps_to + (0,)), 1 - core).wait_recv()
            take([chip_of(0, dx, dy) for dx, dy in what])

    lax.fori_loop(1, chans, level_wait, 0)

    @pl.loop(0, chans // 2)
    def _(pair):
        table[:, pl.ds(pl.multiple_of(pair * 128, 128), 128)] = terms[2 * pair] + terms[2 * pair + 1]

    steps = top - bottom + 1

    def weigh(product, point, columns):
        weighted[:, columns] = (product * pot_ref[pl.ds(rows_ref[point], 1), columns]).astype(jnp.bfloat16)

    for begin in range(0, n, TILE):
        weigh(summed[:, pl.ds(begin, TILE)], top - 1, pl.ds(begin, TILE))

    def pass_on():
        pltpu.make_async_remote_copy(
            src_ref=message, dst_ref=wave_slot(me), send_sem=hop_send.at[0], recv_sem=hop_recv,
            device_id=(previous, me), device_id_type=MESH,
        ).wait_recv()
        to_peers(wave_copy)

    def back(step, carry):
        point = top - step

        @pl.when(jnp.logical_and(step == pass_at, first > 0))
        def _():
            pass_on()

        current, other = lax.rem(step, 2), 1 - lax.rem(step, 2)
        for begin in range(0, n, TILE):
            columns = pl.ds(begin, TILE)
            product = jnp.dot(weighted[...], flipped[:, columns], preferred_element_type=jnp.float32)
            new = (
                level_of(point, table[0:1, columns], table[1:2, columns]) * state[current, :, columns]
                - state[other, :, columns] - step_square * product
            )
            state[other, :, columns] = new
            rounded[:, columns] = new.astype(jnp.bfloat16)

        @pl.when(step + 1 < steps)
        def _():
            for begin in range(0, n, TILE):
                columns = pl.ds(begin, TILE)
                weigh(
                    jnp.dot(rounded[...], basis[:, columns], preferred_element_type=jnp.float32),
                    point - 1, columns,
                )

        return carry

    lax.fori_loop(1, steps, back, 0)

    @pl.when(jnp.logical_and(steps <= pass_at, first > 0))
    def _():
        pass_on()

    newest, older = lax.rem(steps, 2), 1 - lax.rem(steps, 2)

    def differences(rows):
        return jnp.concatenate([rows[:width], rows[:width] - rows[width:]], axis=0)

    @pl.loop(0, chans // 4)
    def _(quarter):
        for part in range(2):
            pair = 2 * quarter + part
            columns = pl.ds(pl.multiple_of(pair * 128, 128), 128)
            before = differences(state[older, :, columns])
            main = differences(state[newest, :, columns]) - before
            main, before = (jnp.transpose(v.astype(jnp.bfloat16)) for v in (main, before))
            for side in range(2):
                place = pl.ds(pl.multiple_of((2 * pair + side) * 128, 128), 128)
                lines = slice(side * width, (side + 1) * width)
                turned[place, :] = jnp.concatenate([main[lines], before[lines]], axis=0)

    def wave_wait(distance, carry):
        owner = lax.rem(me + distance, chans)
        pltpu.make_async_remote_copy(
            src_ref=wave_slot(owner), dst_ref=wave_slot(owner),
            send_sem=wave_send.at[owner], recv_sem=wave_recv.at[owner],
            device_id=(sector, owner), device_id_type=MESH,
        ).wait_recv()
        return carry

    lax.fori_loop(1, chans, wave_wait, 0)
    result = jnp.dot(whole[...], turned[...], preferred_element_type=jnp.float32)
    swapped = pltpu.roll(result, width, 1)

    def hop_copy(step):
        return pltpu.make_async_remote_copy(
            src_ref=message, dst_ref=wave_slot(me), send_sem=hop_send.at[step], recv_sem=hop_recv,
            device_id=(sector + 1 + step, me), device_id_type=MESH,
        )

    @pl.when(sends)
    def _():
        message[...] = result.astype(jnp.bfloat16)

        def go(step, carry):
            hop_copy(following - 1 - step).start()
            return carry

        lax.fori_loop(0, following, go, 0)

        def done(step, carry):
            hop_copy(step).wait_send()
            return carry

        lax.fori_loop(0, following, done, 0)

    out_ref[0] = (result - swapped)[:, :width]
    out_ref[1] = result[:, :width]
    sent_to_peers(level_copy)
    sent_to_peers(wave_copy)
    for half in (0, 1):
        for part, toward, target in OWN_TO:
            ring_copy(half, None, toward, target, own_part(half, part)).wait_send()
        for slot in range(OWN):
            for toward, target in FORWARD[slot]:
                ring_copy(half, slot, toward, target).wait_send()
            if slot % 2 == 0:
                twin_copy(half, slot, core).wait_send()
    own_twin_copy(me).wait_send()


def local(angular, potential, point_rows, quanta, start_waves):
    chans, sectors = lax.axis_size("chan"), lax.axis_size("sector")
    points, n = angular.shape[0], angular.shape[1] * chans
    solutions, width = start_waves.shape
    vmem, hbm = pl.BlockSpec(memory_space=pltpu.VMEM), pl.BlockSpec(memory_space=pltpu.HBM)
    return pl.pallas_call(
        functools.partial(kernel, chans, sectors),
        out_shape=jax.ShapeDtypeStruct((2, solutions, width), jnp.float32),
        in_specs=[
            hbm,
            pl.BlockSpec(memory_space=pltpu.SMEM),
            hbm, hbm, hbm,
        ],
        out_specs=vmem,
        scratch_shapes=[
            pltpu.VMEM(potential.shape, jnp.float32),
            pltpu.VMEM(quanta.shape, jnp.int32),
            pltpu.VMEM(start_waves.shape, jnp.float32),
            pltpu.VMEM((n, points), jnp.bfloat16),
            pltpu.VMEM((points, n), jnp.bfloat16),
            pltpu.VMEM((2, 2 * width, n), jnp.float32),
            pltpu.VMEM((2 * width, n), jnp.bfloat16),
            pltpu.VMEM((2 * width, points), jnp.bfloat16),
            pltpu.VMEM((2 * width, points), jnp.float32),
            pltpu.VMEM((2 * n, 2 * width), jnp.bfloat16),
            pltpu.VMEM((solutions, 2 * n), jnp.bfloat16),
            pltpu.VMEM((solutions, 2 * width), jnp.bfloat16),
            pltpu.VMEM((chans, 8, 2 * width), jnp.float32),
            pltpu.VMEM((8, n), jnp.float32),
            pltpu.SemaphoreType.DMA((chans,)),
            pltpu.SemaphoreType.DMA((chans,)),
            pltpu.SemaphoreType.DMA((chans,)),
            pltpu.SemaphoreType.DMA((chans,)),
            pltpu.SemaphoreType.DMA((max(GROUPS),)),
            pltpu.SemaphoreType.DMA,
            pltpu.SemaphoreType.DMA((2, OWN)),
            pltpu.SemaphoreType.DMA((2, OWN)),
            pltpu.SemaphoreType.DMA((2, OWN // 2 + 1)),
            pltpu.SemaphoreType.DMA((2, OWN // 2 + 1)),
            pltpu.SemaphoreType.DMA((4,)),
        ],
        compiler_params=pltpu.CompilerParams(
            collective_id=0, has_side_effects=True, vmem_limit_bytes=60 * 1024 * 1024
        ),
    )(angular.T, point_rows, potential, quanta, start_waves)


def solution(mesh):
    placed = (P(None, "chan"), P(), P(), P(None, "chan"), P(None, "chan"))
    return jax.shard_map(
        local, mesh=mesh, in_specs=placed, out_specs=P("sector", None, "chan"), check_vma=False
    )
```

```python
import functools

import jax
import jax.numpy as jnp
from jax import lax
from jax.experimental import pallas as pl
from jax.experimental.pallas import tpu as pltpu
from jax.sharding import PartitionSpec as P

energy = 3.5
rotor_const = 0.02
radius_first = 8.0
radius_step = 0.5
step_square = 0.08

GROUPS = (2, 3, 5, 6)
PASS_AT = (99, 99, 99, 99)
TILE = 512
MESH = pl.DeviceIdType.MESH

SIDE = 4
STEPS = (0, -1, 1, 2)
PIECES = [(f, s, part) for f in STEPS for s in STEPS if (f, s) != (0, 0) for part in (0, 1)]
OWN = len(PIECES)
FORE, BACK, UP, DOWN = (1, 0), (-1, 0), (0, 1), (0, -1)
OWN_TO = [
    (part, toward, PIECES.index((-toward[0], -toward[1], part)))
    for turn in (0, 1)
    for toward, early in ((FORE, 0), (BACK, 1), (UP, 0), (DOWN, 1))
    for part in (early if turn == 0 else 1 - early,)
]


def sent_on(piece):
    f, s, part = piece
    result = []
    if s == 0:
        if (f, part) == (-1, 0):
            result.append((FORE, PIECES.index((2, 0, 0))))
        if (f, part) == (1, 1):
            result.append((BACK, PIECES.index((2, 0, 1))))
        result += [(UP, PIECES.index((f, -1, part))), (DOWN, PIECES.index((f, 1, part)))]
    if (s, part) == (-1, 0):
        result.append((UP, PIECES.index((f, 2, 0))))
    if (s, part) == (1, 1):
        result.append((DOWN, PIECES.index((f, 2, 1))))
    return result


FORWARD = [sent_on(piece) for piece in PIECES]
FAR_FIRST = sorted(
    [(dx, dy) for dx in STEPS for dy in STEPS if (dx, dy) != (0, 0)], key=lambda o: -abs(o[0]) - abs(o[1])
)
ORDER = [
    ("pieces", [(-1, 0, 0), (1, 0, 1), (0, -1, 0), (0, 1, 1), (-1, 0, 1), (1, 0, 0), (0, -1, 1), (0, 1, 0)]),
    ("levels", 0), ("take", [(0, 0)]),
    ("pieces", [(2, 0, 0), (2, 0, 1), (-1, -1, 0), (1, -1, 0), (-1, 1, 1), (1, 1, 1)]),
    ("levels", 1), ("take", [(-1, 0), (0, -1)]),
    ("pieces", [(0, 2, 0), (0, 2, 1), (-1, -1, 1), (1, -1, 1), (-1, 1, 0), (1, 1, 0)]),
    ("take", [(1, 0), (0, 1)]),
    ("pieces", [(2, -1, 0), (2, 1, 1)]), ("take", [(-1, -1), (1, -1)]),
    ("pieces", [(2, -1, 1), (2, 1, 0)]), ("take", [(-1, 1), (1, 1)]),
    ("pieces", [(-1, 2, 0), (-1, 2, 1)]), ("take", [(2, 0), (0, 2)]),
    ("pieces", [(1, 2, 0), (1, 2, 1)]), ("take", [(2, -1), (-1, 2)]),
    ("waves", 0), ("waves", 1), ("take", [(2, 1), (1, 2)]), ("pieces", [(2, 2, 0), (2, 2, 1)]), ("take", [(2, 2)]),
]


def pick(index, values):
    result = values[-1]
    for place in range(len(values) - 1):
        result = jnp.where(index == place, values[place], result)
    return result


def kernel(
    chans, sectors,
    mine_ref, rows_ref, pot_in, quanta_in, start_in, out_ref,
    pot_ref, quanta_ref, start_ref,
    basis, flipped, state, rounded, weighted, summed, turned,
    whole, message, terms, table, level_send, level_recv, wave_send, wave_recv, hop_send, hop_recv,
    ring_send, ring_recv, twin_send, twin_recv, load_sem,
):
    n = basis.shape[0]
    width = n // chans
    sector, me = lax.axis_index("sector"), lax.axis_index("chan")
    first_of, last_of, next_of, pass_of = [], [], [], []
    start = 0
    for index, size in enumerate(GROUPS):
        following = GROUPS[index + 1] if index + 1 < len(GROUPS) else 0
        for _ in range(size):
            first_of.append(start)
            last_of.append(start + size - 1)
            next_of.append(following)
            pass_of.append(PASS_AT[index])
        start += size
    first = pick(sector, first_of)
    last = pick(sector, last_of)
    following = pick(sector, next_of)
    pass_at = pick(sector, pass_of)
    sends = jnp.logical_and(sector == last, following > 0)
    previous = first - 1

    core, y_at, x_at = lax.rem(me, 2), lax.rem(me // 2, SIDE), me // (2 * SIDE)
    twin = me + 1 - 2 * core
    cut = n // 2
    own_rows = pl.ds(pl.multiple_of(me * width, width), width)
    loads = [
        pltpu.make_async_copy(source, place, load_sem.at[index])
        for index, (source, place) in enumerate([
            (quanta_in, quanta_ref), (start_in, start_ref), (mine_ref, basis.at[own_rows, :]), (pot_in, pot_ref),
        ])
    ]
    for load in loads:
        load.start()

    barrier = pltpu.get_barrier_semaphore()

    def greet(distance, carry):
        peer = lax.rem(me + distance, chans)
        pl.semaphore_signal(barrier, inc=1, device_id=(sector, peer), device_id_type=MESH)
        return carry

    lax.fori_loop(1, chans, greet, 0)

    @pl.when(sends)
    def _():
        def greet_next(step, carry):
            pl.semaphore_signal(barrier, inc=1, device_id=(sector + 1 + step, me), device_id_type=MESH)
            return carry

        lax.fori_loop(0, following, greet_next, 0)

    @pl.when(first > 0)
    def _():
        pl.semaphore_signal(barrier, inc=1, device_id=(previous, me), device_id_type=MESH)

    greeted = chans - 1 + jnp.where(sends, following, 0) + jnp.where(first > 0, 1, 0)
    pl.semaphore_wait(barrier, greeted)

    def level_copy(peer):
        return pltpu.make_async_remote_copy(
            src_ref=terms.at[me], dst_ref=terms.at[me],
            send_sem=level_send, recv_sem=level_recv,
            device_id=(sector, peer), device_id_type=MESH,
        )

    def wave_slot(owner):
        return whole.at[:, pl.ds(pl.multiple_of(owner * 2 * width, 2 * width), 2 * width)]

    def wave_copy(peer):
        return pltpu.make_async_remote_copy(
            src_ref=wave_slot(me), dst_ref=wave_slot(me),
            send_sem=wave_send, recv_sem=wave_recv,
            device_id=(sector, peer), device_id_type=MESH,
        )

    def to_peers(make, portion=None):
        for place, (dx, dy) in enumerate(FAR_FIRST):
            if portion in (None, place % 2):
                for side in (0, 1):
                    make(chip_of(0, dx, dy) * 2 + side).start()
        if portion != 0:
            make(twin).start()

    def chip_of(half, first_step, second_step):
        dx, dy = (first_step, second_step) if half == 0 else (second_step, first_step)
        return lax.rem(x_at + dx + SIDE, SIDE) * SIDE + lax.rem(y_at + dy + SIDE, SIDE)

    def piece(half, owner, part):
        begin, size = (0, width) if part is None else (part * (width // 2), width // 2)
        rows = pl.ds(pl.multiple_of(owner * width + begin, width // 2), size)
        return basis.at[rows, pl.ds(half * cut, cut)]

    def ring_copy(half, slot, toward, target, source=None):
        first_step, second_step, part = (0, 0, PIECES[target][2]) if slot is None else PIECES[slot]
        owner = chip_of(half, first_step, second_step) * 2 + core
        return pltpu.make_async_remote_copy(
            src_ref=piece(half, owner, part) if source is None else source,
            dst_ref=piece(half, owner, part),
            send_sem=ring_send, recv_sem=ring_recv.at[half, target],
            device_id=(sector, chip_of(half, *toward) * 2 + core), device_id_type=MESH,
        )

    def twin_copy(half, slot, side):
        first_step, second_step, _ = PIECES[slot]
        place = piece(half, chip_of(half, first_step, second_step) * 2 + side, None)
        return pltpu.make_async_remote_copy(
            src_ref=place, dst_ref=place,
            send_sem=twin_send, recv_sem=twin_recv.at[half, slot // 2],
            device_id=(sector, twin), device_id_type=MESH,
        )

    def arrived(half, slot, both):
        pltpu.make_async_remote_copy(
            src_ref=mine_ref.at[pl.ds(0, width // 2), pl.ds(0, cut)], dst_ref=piece(
                half, chip_of(half, *PIECES[slot][:2]) * 2 + core, PIECES[slot][2]
            ),
            send_sem=ring_send, recv_sem=ring_recv.at[half, slot],
            device_id=(sector, twin), device_id_type=MESH,
        ).wait_recv()
        for toward, target in FORWARD[slot]:
            ring_copy(half, slot, toward, target).start()
        if both:
            twin_copy(half, slot, core).start()

    def own_twin_copy(owner):
        place = basis.at[pl.ds(pl.multiple_of(owner * width, width), width), :]
        return pltpu.make_async_remote_copy(
            src_ref=mine_ref, dst_ref=place, send_sem=twin_send, recv_sem=twin_recv.at[0, OWN // 2],
            device_id=(sector, twin), device_id_type=MESH,
        )

    def own_part(half, part):
        return mine_ref.at[pl.ds(part * (width // 2), width // 2), pl.ds(half * cut, cut)]

    for part, toward, target in OWN_TO:
        for half in (0, 1):
            ring_copy(half, None, toward, target, own_part(half, part)).start()
    own_twin_copy(me).start()

    loads[0].wait()
    quanta = quanta_ref[...].astype(jnp.float32)
    j_values, l_values = quanta[0:1, :], quanta[1:2, :]
    a_row = 2.0 - step_square * (energy - rotor_const * j_values * (j_values + 1.0))
    b_row = step_square * (l_values * (l_values + 1.0))
    ab = jnp.concatenate([a_row, b_row, jnp.zeros((6, width), jnp.float32)], axis=0)
    lane = lax.broadcasted_iota(jnp.int32, (8, 2 * width), 1)
    half = lane // width
    terms[me] = jnp.where(half == lax.rem(me, 2), jnp.concatenate([ab, ab], axis=1), 0.0)
    loads[1].wait()

    @pl.when(first == 0)
    def _():
        waves = start_ref[...].astype(jnp.bfloat16)
        whole[:, pl.ds(pl.multiple_of(me * 2 * width, 2 * width), 2 * width)] = jnp.concatenate(
            [waves, waves], axis=1
        )

    top = 2 * sector + 1
    bottom = 2 * first
    top_row = rows_ref[top]
    loads[2].wait()
    loads[3].wait()
    weighted[pl.ds(0, width), :] = (
        basis[own_rows, :].astype(jnp.float32) * pot_ref[pl.ds(top_row, 1), :]
    ).astype(jnp.bfloat16)
    summed[...] = jnp.zeros_like(summed)

    def level_of(point, a_row, b_row):
        radius = jnp.full(a_row.shape, radius_first, jnp.float32) + radius_step * point.astype(jnp.float32)
        return a_row + b_row * (1.0 / (radius * radius))

    own_level = level_of(top, terms[me, 0:1, :], terms[me, 1:2, :])

    def take(chips):
        places, news = [], []
        for chip in chips:
            columns = pl.ds(pl.multiple_of(chip * 128, 128), 128)
            for begin in range(0, n, TILE):
                flipped[pl.ds(begin, TILE), columns] = jnp.transpose(basis[columns, pl.ds(begin, TILE)])
            places.append(columns)
        for chip, columns in zip(chips, places):
            product = jnp.dot(
                weighted[pl.ds(0, width), :], flipped[:, columns], preferred_element_type=jnp.float32
            )
            row = lax.broadcasted_iota(jnp.int32, (width, 128), 0)
            column = lax.broadcasted_iota(jnp.int32, (width, 128), 1) + chip * 128
            own = jnp.where(column == me * width + row, 1.0, 0.0)
            both = jnp.concatenate([own_level * own - step_square * product, own], axis=0)
            state[0, :, columns] = jnp.concatenate([own, jnp.zeros_like(own)], axis=0)
            state[1, :, columns] = both
            news.append(both.astype(jnp.bfloat16))
        for begin in range(0, n, TILE):
            tile = pl.ds(begin, TILE)
            total = summed[:, tile]
            for columns, both in zip(places, news):
                total += jnp.dot(both, basis[columns, tile], preferred_element_type=jnp.float32)
            summed[:, tile] = total

    handed = ([], [])
    for kind, what in ORDER:
        if kind == "pieces":
            for name in what:
                for half in (0, 1):
                    handed[half].append(name)
                    arrived(half, PIECES.index(name), name[:2] + (1 - name[2],) in handed[half])
        elif kind == "levels":
            to_peers(level_copy, what)
        elif kind == "waves":
            @pl.when(first == 0)
            def _(portion=what):
                to_peers(wave_copy, portion)
        else:
            for dx, dy in what:
                if (dx, dy) == (0, 0):
                    own_twin_copy(twin).wait_recv()
                else:
                    for half, steps_to in ((0, (dx, dy)), (1, (dy, dx))):
                        twin_copy(half, PIECES.index(steps_to + (0,)), 1 - core).wait_recv()
            take([chip_of(0, dx, dy) for dx, dy in what])

    def all_of(place, send_sem, recv_sem):
        return pltpu.make_async_remote_copy(
            src_ref=place, dst_ref=place, send_sem=send_sem, recv_sem=recv_sem,
            device_id=(sector, twin), device_id_type=MESH,
        )

    levels = all_of(terms.at[pl.ds(0, chans - 1)], level_send, level_recv)
    levels.wait_recv()

    @pl.loop(0, chans // 2)
    def _(pair):
        table[:, pl.ds(pl.multiple_of(pair * 128, 128), 128)] = terms[2 * pair] + terms[2 * pair + 1]

    steps = top - bottom + 1

    def weigh(product, point, columns):
        weighted[:, columns] = (product * pot_ref[pl.ds(rows_ref[point], 1), columns]).astype(jnp.bfloat16)

    for begin in range(0, n, TILE):
        weigh(summed[:, pl.ds(begin, TILE)], top - 1, pl.ds(begin, TILE))

    def pass_on():
        pltpu.make_async_remote_copy(
            src_ref=message, dst_ref=wave_slot(me), send_sem=hop_send.at[0], recv_sem=hop_recv,
            device_id=(previous, me), device_id_type=MESH,
        ).wait_recv()
        to_peers(wave_copy)

    def back(step, carry):
        point = top - step

        @pl.when(jnp.logical_and(step == pass_at, first > 0))
        def _():
            pass_on()

        current, other = lax.rem(step, 2), 1 - lax.rem(step, 2)
        for begin in range(0, n, TILE):
            columns = pl.ds(begin, TILE)
            product = jnp.dot(weighted[...], flipped[:, columns], preferred_element_type=jnp.float32)
            new = (
                level_of(point, table[0:1, columns], table[1:2, columns]) * state[current, :, columns]
                - state[other, :, columns] - step_square * product
            )
            state[other, :, columns] = new
            rounded[:, columns] = new.astype(jnp.bfloat16)

        @pl.when(step + 1 < steps)
        def _():
            for begin in range(0, n, TILE):
                columns = pl.ds(begin, TILE)
                weigh(
                    jnp.dot(rounded[...], basis[:, columns], preferred_element_type=jnp.float32),
                    point - 1, columns,
                )

        return carry

    lax.fori_loop(1, steps, back, 0)

    @pl.when(jnp.logical_and(steps <= pass_at, first > 0))
    def _():
        pass_on()

    newest, older = lax.rem(steps, 2), 1 - lax.rem(steps, 2)

    def differences(rows):
        return jnp.concatenate([rows[:width], rows[:width] - rows[width:]], axis=0)

    @pl.loop(0, chans // 4)
    def _(quarter):
        for part in range(2):
            pair = 2 * quarter + part
            columns = pl.ds(pl.multiple_of(pair * 128, 128), 128)
            before = differences(state[older, :, columns])
            main = differences(state[newest, :, columns]) - before
            main, before = (jnp.transpose(v.astype(jnp.bfloat16)) for v in (main, before))
            for side in range(2):
                place = pl.ds(pl.multiple_of((2 * pair + side) * 128, 128), 128)
                lines = slice(side * width, (side + 1) * width)
                turned[place, :] = jnp.concatenate([main[lines], before[lines]], axis=0)

    waves = all_of(whole.at[:, pl.ds(0, (chans - 1) * 2 * width)], wave_send, wave_recv)
    waves.wait_recv()
    result = jnp.dot(whole[...], turned[...], preferred_element_type=jnp.float32)
    swapped = pltpu.roll(result, width, 1)

    def hop_copy(step):
        return pltpu.make_async_remote_copy(
            src_ref=message, dst_ref=wave_slot(me), send_sem=hop_send.at[step], recv_sem=hop_recv,
            device_id=(sector + 1 + step, me), device_id_type=MESH,
        )

    @pl.when(sends)
    def _():
        message[...] = result.astype(jnp.bfloat16)

        def go(step, carry):
            hop_copy(following - 1 - step).start()
            return carry

        lax.fori_loop(0, following, go, 0)

        def done(step, carry):
            hop_copy(step).wait_send()
            return carry

        lax.fori_loop(0, following, done, 0)

    out_ref[0] = (result - swapped)[:, :width]
    out_ref[1] = result[:, :width]
    levels.wait_send()
    waves.wait_send()
    all_of(basis.at[pl.ds(0, n // 2 * OWN // (OWN + 2)), :], ring_send, hop_recv).wait_send()
    all_of(basis.at[pl.ds(0, n // 2), :], twin_send, hop_recv).wait_send()


def local(angular, potential, point_rows, quanta, start_waves):
    chans, sectors = lax.axis_size("chan"), lax.axis_size("sector")
    points, n = angular.shape[0], angular.shape[1] * chans
    solutions, width = start_waves.shape
    vmem, hbm = pl.BlockSpec(memory_space=pltpu.VMEM), pl.BlockSpec(memory_space=pltpu.HBM)
    return pl.pallas_call(
        functools.partial(kernel, chans, sectors),
        out_shape=jax.ShapeDtypeStruct((2, solutions, width), jnp.float32),
        in_specs=[
            hbm,
            pl.BlockSpec(memory_space=pltpu.SMEM),
            hbm, hbm, hbm,
        ],
        out_specs=vmem,
        scratch_shapes=[
            pltpu.VMEM(potential.shape, jnp.float32),
            pltpu.VMEM(quanta.shape, jnp.int32),
            pltpu.VMEM(start_waves.shape, jnp.float32),
            pltpu.VMEM((n, points), jnp.bfloat16),
            pltpu.VMEM((points, n), jnp.bfloat16),
            pltpu.VMEM((2, 2 * width, n), jnp.float32),
            pltpu.VMEM((2 * width, n), jnp.bfloat16),
            pltpu.VMEM((2 * width, points), jnp.bfloat16),
            pltpu.VMEM((2 * width, points), jnp.float32),
            pltpu.VMEM((2 * n, 2 * width), jnp.bfloat16),
            pltpu.VMEM((solutions, 2 * n), jnp.bfloat16),
            pltpu.VMEM((solutions, 2 * width), jnp.bfloat16),
            pltpu.VMEM((chans, 8, 2 * width), jnp.float32),
            pltpu.VMEM((8, n), jnp.float32),
            pltpu.SemaphoreType.DMA,
            pltpu.SemaphoreType.DMA,
            pltpu.SemaphoreType.DMA,
            pltpu.SemaphoreType.DMA,
            pltpu.SemaphoreType.DMA((max(GROUPS),)),
            pltpu.SemaphoreType.DMA,
            pltpu.SemaphoreType.DMA,
            pltpu.SemaphoreType.DMA((2, OWN)),
            pltpu.SemaphoreType.DMA,
            pltpu.SemaphoreType.DMA((2, OWN // 2 + 1)),
            pltpu.SemaphoreType.DMA((4,)),
        ],
        compiler_params=pltpu.CompilerParams(
            collective_id=0, has_side_effects=True, vmem_limit_bytes=60 * 1024 * 1024
        ),
    )(angular.T, point_rows, potential, quanta, start_waves)


def solution(mesh):
    placed = (P(None, "chan"), P(), P(), P(None, "chan"), P(None, "chan"))
    return jax.shard_map(
        local, mesh=mesh, in_specs=placed, out_specs=P("sector", None, "chan"), check_vma=False
    )
```

```python
import functools

import jax
import jax.numpy as jnp
from jax import lax
from jax.experimental import pallas as pl
from jax.experimental.pallas import tpu as pltpu
from jax.sharding import PartitionSpec as P

energy = 3.5
rotor_const = 0.02
radius_first = 8.0
radius_step = 0.5
step_square = 0.08

GROUPS = (2, 3, 5, 6)
PASS_AT = (99, 5, 9, 99)
TILE = 512
MESH = pl.DeviceIdType.MESH

SIDE = 4
STEPS = (0, -1, 1, 2)
PIECES = [(f, s, part) for f in STEPS for s in STEPS if (f, s) != (0, 0) for part in (0, 1)]
OWN = len(PIECES)
FORE, BACK, UP, DOWN = (1, 0), (-1, 0), (0, 1), (0, -1)
OWN_TO = [
    (part, toward, PIECES.index((-toward[0], -toward[1], part)))
    for turn in (0, 1)
    for toward, early in ((FORE, 0), (BACK, 1), (UP, 0), (DOWN, 1))
    for part in (early if turn == 0 else 1 - early,)
]


def sent_on(piece):
    f, s, part = piece
    result = []
    if s == 0:
        if (f, part) == (-1, 0):
            result.append((FORE, PIECES.index((2, 0, 0))))
        if (f, part) == (1, 1):
            result.append((BACK, PIECES.index((2, 0, 1))))
        result += [(UP, PIECES.index((f, -1, part))), (DOWN, PIECES.index((f, 1, part)))]
    if (s, part) == (-1, 0):
        result.append((UP, PIECES.index((f, 2, 0))))
    if (s, part) == (1, 1):
        result.append((DOWN, PIECES.index((f, 2, 1))))
    return result


FORWARD = [sent_on(piece) for piece in PIECES]
FAR_FIRST = sorted(
    [(dx, dy) for dx in STEPS for dy in STEPS if (dx, dy) != (0, 0)], key=lambda o: -abs(o[0]) - abs(o[1])
)
ORDER = [
    ("pieces", [(-1, 0, 0), (1, 0, 1), (0, -1, 0), (0, 1, 1), (-1, 0, 1), (1, 0, 0), (0, -1, 1), (0, 1, 0)]),
    ("take", [(0, 0)]),
    ("pieces", [(2, 0, 0), (2, 0, 1), (-1, -1, 0), (1, -1, 0), (-1, 1, 1), (1, 1, 1)]),
    ("take", [(-1, 0), (0, -1)]),
    ("pieces", [(0, 2, 0), (0, 2, 1), (-1, -1, 1), (1, -1, 1), (-1, 1, 0), (1, 1, 0)]),
    ("levels", 0), ("levels", 1), ("take", [(1, 0), (0, 1)]),
    ("pieces", [(2, -1, 0), (2, 1, 1)]), ("take", [(-1, -1), (1, -1)]),
    ("pieces", [(2, -1, 1), (2, 1, 0)]), ("take", [(-1, 1), (1, 1)]),
    ("pieces", [(-1, 2, 0), (-1, 2, 1)]), ("take", [(2, 0), (0, 2)]),
    ("pieces", [(1, 2, 0), (1, 2, 1)]), ("take", [(2, -1), (-1, 2)]),
    ("waves", 0), ("waves", 1), ("take", [(2, 1), (1, 2)]), ("pieces", [(2, 2, 0), (2, 2, 1)]), ("take", [(2, 2)]),
]


def pick(index, values):
    result = values[-1]
    for place in range(len(values) - 1):
        result = jnp.where(index == place, values[place], result)
    return result


def kernel(
    chans, sectors,
    mine_ref, rows_ref, pot_in, quanta_in, start_in, out_ref,
    pot_ref, quanta_ref, start_ref,
    basis, flipped, state, rounded, weighted, summed, turned,
    whole, message, terms, table, level_send, level_recv, wave_send, wave_recv, hop_send, hop_recv,
    ring_send, ring_recv, twin_send, twin_recv, load_sem,
):
    n = basis.shape[0]
    width = n // chans
    sector, me = lax.axis_index("sector"), lax.axis_index("chan")
    first_of, last_of, next_of, pass_of = [], [], [], []
    start = 0
    for index, size in enumerate(GROUPS):
        following = GROUPS[index + 1] if index + 1 < len(GROUPS) else 0
        for _ in range(size):
            first_of.append(start)
            last_of.append(start + size - 1)
            next_of.append(following)
            pass_of.append(PASS_AT[index])
        start += size
    first = pick(sector, first_of)
    last = pick(sector, last_of)
    following = pick(sector, next_of)
    pass_at = pick(sector, pass_of)
    sends = jnp.logical_and(sector == last, following > 0)
    previous = first - 1

    core, y_at, x_at = lax.rem(me, 2), lax.rem(me // 2, SIDE), me // (2 * SIDE)
    twin = me + 1 - 2 * core
    cut = n // 2
    own_rows = pl.ds(pl.multiple_of(me * width, width), width)
    loads = [
        pltpu.make_async_copy(source, place, load_sem.at[index])
        for index, (source, place) in enumerate([
            (quanta_in, quanta_ref), (start_in, start_ref), (mine_ref, basis.at[own_rows, :]), (pot_in, pot_ref),
        ])
    ]
    for load in loads:
        load.start()

    barrier = pltpu.get_barrier_semaphore()

    def greet(distance, carry):
        peer = lax.rem(me + distance, chans)
        pl.semaphore_signal(barrier, inc=1, device_id=(sector, peer), device_id_type=MESH)
        return carry

    lax.fori_loop(1, chans, greet, 0)

    @pl.when(sends)
    def _():
        def greet_next(step, carry):
            pl.semaphore_signal(barrier, inc=1, device_id=(sector + 1 + step, me), device_id_type=MESH)
            return carry

        lax.fori_loop(0, following, greet_next, 0)

    @pl.when(first > 0)
    def _():
        pl.semaphore_signal(barrier, inc=1, device_id=(previous, me), device_id_type=MESH)

    greeted = chans - 1 + jnp.where(sends, following, 0) + jnp.where(first > 0, 1, 0)
    pl.semaphore_wait(barrier, greeted)

    def level_copy(peer):
        return pltpu.make_async_remote_copy(
            src_ref=terms.at[me], dst_ref=terms.at[me],
            send_sem=level_send, recv_sem=level_recv,
            device_id=(sector, peer), device_id_type=MESH,
        )

    def wave_slot(owner):
        return whole.at[:, pl.ds(pl.multiple_of(owner * 2 * width, 2 * width), 2 * width)]

    def wave_copy(peer):
        return pltpu.make_async_remote_copy(
            src_ref=wave_slot(me), dst_ref=wave_slot(me),
            send_sem=wave_send, recv_sem=wave_recv,
            device_id=(sector, peer), device_id_type=MESH,
        )

    def to_peers(make, portion=None):
        for place, (dx, dy) in enumerate(FAR_FIRST):
            if portion in (None, place % 2):
                for side in (0, 1):
                    make(chip_of(0, dx, dy) * 2 + side).start()
        if portion != 0:
            make(twin).start()

    def chip_of(half, first_step, second_step):
        dx, dy = (first_step, second_step) if half == 0 else (second_step, first_step)
        return lax.rem(x_at + dx + SIDE, SIDE) * SIDE + lax.rem(y_at + dy + SIDE, SIDE)

    def piece(half, owner, part):
        begin, size = (0, width) if part is None else (part * (width // 2), width // 2)
        rows = pl.ds(pl.multiple_of(owner * width + begin, width // 2), size)
        return basis.at[rows, pl.ds(half * cut, cut)]

    def ring_copy(half, slot, toward, target, source=None):
        first_step, second_step, part = (0, 0, PIECES[target][2]) if slot is None else PIECES[slot]
        owner = chip_of(half, first_step, second_step) * 2 + core
        return pltpu.make_async_remote_copy(
            src_ref=piece(half, owner, part) if source is None else source,
            dst_ref=piece(half, owner, part),
            send_sem=ring_send, recv_sem=ring_recv.at[half, target],
            device_id=(sector, chip_of(half, *toward) * 2 + core), device_id_type=MESH,
        )

    def twin_copy(half, slot, side):
        first_step, second_step, _ = PIECES[slot]
        place = piece(half, chip_of(half, first_step, second_step) * 2 + side, None)
        return pltpu.make_async_remote_copy(
            src_ref=place, dst_ref=place,
            send_sem=twin_send, recv_sem=twin_recv.at[half, slot // 2],
            device_id=(sector, twin), device_id_type=MESH,
        )

    def arrived(half, slot, both):
        pltpu.make_async_remote_copy(
            src_ref=mine_ref.at[pl.ds(0, width // 2), pl.ds(0, cut)], dst_ref=piece(
                half, chip_of(half, *PIECES[slot][:2]) * 2 + core, PIECES[slot][2]
            ),
            send_sem=ring_send, recv_sem=ring_recv.at[half, slot],
            device_id=(sector, twin), device_id_type=MESH,
        ).wait_recv()
        for toward, target in FORWARD[slot]:
            ring_copy(half, slot, toward, target).start()
        if both:
            twin_copy(half, slot, core).start()

    def own_twin_copy(owner):
        place = basis.at[pl.ds(pl.multiple_of(owner * width, width), width), :]
        return pltpu.make_async_remote_copy(
            src_ref=mine_ref, dst_ref=place, send_sem=twin_send, recv_sem=twin_recv.at[0, OWN // 2],
            device_id=(sector, twin), device_id_type=MESH,
        )

    def own_part(half, part):
        return mine_ref.at[pl.ds(part * (width // 2), width // 2), pl.ds(half * cut, cut)]

    for part, toward, target in OWN_TO:
        for half in (0, 1):
            ring_copy(half, None, toward, target, own_part(half, part)).start()
    own_twin_copy(me).start()

    loads[0].wait()
    quanta = quanta_ref[...].astype(jnp.float32)
    j_values, l_values = quanta[0:1, :], quanta[1:2, :]
    a_row = 2.0 - step_square * (energy - rotor_const * j_values * (j_values + 1.0))
    b_row = step_square * (l_values * (l_values + 1.0))
    ab = jnp.concatenate([a_row, b_row, jnp.zeros((6, width), jnp.float32)], axis=0)
    lane = lax.broadcasted_iota(jnp.int32, (8, 2 * width), 1)
    half = lane // width
    terms[me] = jnp.where(half == lax.rem(me, 2), jnp.concatenate([ab, ab], axis=1), 0.0)
    loads[1].wait()

    @pl.when(first == 0)
    def _():
        waves = start_ref[...].astype(jnp.bfloat16)
        whole[:, pl.ds(pl.multiple_of(me * 2 * width, 2 * width), 2 * width)] = jnp.concatenate(
            [waves, waves], axis=1
        )

    top = 2 * sector + 1
    bottom = 2 * first
    top_row = rows_ref[top]
    loads[2].wait()
    loads[3].wait()
    weighted[pl.ds(0, width), :] = (
        basis[own_rows, :].astype(jnp.float32) * pot_ref[pl.ds(top_row, 1), :]
    ).astype(jnp.bfloat16)
    summed[...] = jnp.zeros_like(summed)

    def level_of(point, a_row, b_row):
        radius = jnp.full(a_row.shape, radius_first, jnp.float32) + radius_step * point.astype(jnp.float32)
        return a_row + b_row * (1.0 / (radius * radius))

    own_level = level_of(top, terms[me, 0:1, :], terms[me, 1:2, :])

    def take(chips):
        places, news = [], []
        for chip in chips:
            columns = pl.ds(pl.multiple_of(chip * 128, 128), 128)
            for begin in range(0, n, TILE):
                flipped[pl.ds(begin, TILE), columns] = jnp.transpose(basis[columns, pl.ds(begin, TILE)])
            places.append(columns)
        for chip, columns in zip(chips, places):
            product = jnp.dot(
                weighted[pl.ds(0, width), :], flipped[:, columns], preferred_element_type=jnp.float32
            )
            row = lax.broadcasted_iota(jnp.int32, (width, 128), 0)
            column = lax.broadcasted_iota(jnp.int32, (width, 128), 1) + chip * 128
            own = jnp.where(column == me * width + row, 1.0, 0.0)
            both = jnp.concatenate([own_level * own - step_square * product, own], axis=0)
            state[0, :, columns] = jnp.concatenate([own, jnp.zeros_like(own)], axis=0)
            state[1, :, columns] = both
            news.append(both.astype(jnp.bfloat16))
        for begin in range(0, n, TILE):
            tile = pl.ds(begin, TILE)
            total = summed[:, tile]
            for columns, both in zip(places, news):
                total += jnp.dot(both, basis[columns, tile], preferred_element_type=jnp.float32)
            summed[:, tile] = total

    handed = ([], [])
    for kind, what in ORDER:
        if kind == "pieces":
            for name in what:
                for half in (0, 1):
                    handed[half].append(name)
                    arrived(half, PIECES.index(name), name[:2] + (1 - name[2],) in handed[half])
        elif kind == "levels":
            to_peers(level_copy, what)
        elif kind == "waves":
            @pl.when(first == 0)
            def _(portion=what):
                to_peers(wave_copy, portion)
        else:
            for dx, dy in what:
                if (dx, dy) == (0, 0):
                    own_twin_copy(twin).wait_recv()
                else:
                    for half, steps_to in ((0, (dx, dy)), (1, (dy, dx))):
                        twin_copy(half, PIECES.index(steps_to + (0,)), 1 - core).wait_recv()
            take([chip_of(0, dx, dy) for dx, dy in what])

    def all_of(place, send_sem, recv_sem):
        return pltpu.make_async_remote_copy(
            src_ref=place, dst_ref=place, send_sem=send_sem, recv_sem=recv_sem,
            device_id=(sector, twin), device_id_type=MESH,
        )

    levels = all_of(terms.at[pl.ds(0, chans - 1)], level_send, level_recv)
    levels.wait_recv()

    @pl.loop(0, chans // 2)
    def _(pair):
        table[:, pl.ds(pl.multiple_of(pair * 128, 128), 128)] = terms[2 * pair] + terms[2 * pair + 1]

    steps = top - bottom + 1

    def weigh(product, point, columns):
        weighted[:, columns] = (product * pot_ref[pl.ds(rows_ref[point], 1), columns]).astype(jnp.bfloat16)

    for begin in range(0, n, TILE):
        weigh(summed[:, pl.ds(begin, TILE)], top - 1, pl.ds(begin, TILE))

    def pass_on():
        pltpu.make_async_remote_copy(
            src_ref=message, dst_ref=wave_slot(me), send_sem=hop_send.at[0], recv_sem=hop_recv,
            device_id=(previous, me), device_id_type=MESH,
        ).wait_recv()
        to_peers(wave_copy)

    def back(step, carry):
        point = top - step

        @pl.when(jnp.logical_and(step == pass_at, first > 0))
        def _():
            pass_on()

        current, other = lax.rem(step, 2), 1 - lax.rem(step, 2)
        for begin in range(0, n, TILE):
            columns = pl.ds(begin, TILE)
            product = jnp.dot(weighted[...], flipped[:, columns], preferred_element_type=jnp.float32)
            new = (
                level_of(point, table[0:1, columns], table[1:2, columns]) * state[current, :, columns]
                - state[other, :, columns] - step_square * product
            )
            state[other, :, columns] = new
            rounded[:, columns] = new.astype(jnp.bfloat16)

        @pl.when(step + 1 < steps)
        def _():
            for begin in range(0, n, TILE):
                columns = pl.ds(begin, TILE)
                weigh(
                    jnp.dot(rounded[...], basis[:, columns], preferred_element_type=jnp.float32),
                    point - 1, columns,
                )

        return carry

    lax.fori_loop(1, steps, back, 0)

    @pl.when(jnp.logical_and(steps <= pass_at, first > 0))
    def _():
        pass_on()

    newest, older = lax.rem(steps, 2), 1 - lax.rem(steps, 2)

    def differences(rows):
        return jnp.concatenate([rows[:width], rows[:width] - rows[width:]], axis=0)

    @pl.loop(0, chans // 4)
    def _(quarter):
        for part in range(2):
            pair = 2 * quarter + part
            columns = pl.ds(pl.multiple_of(pair * 128, 128), 128)
            before = differences(state[older, :, columns])
            main = differences(state[newest, :, columns]) - before
            main, before = (jnp.transpose(v.astype(jnp.bfloat16)) for v in (main, before))
            for side in range(2):
                place = pl.ds(pl.multiple_of((2 * pair + side) * 128, 128), 128)
                lines = slice(side * width, (side + 1) * width)
                turned[place, :] = jnp.concatenate([main[lines], before[lines]], axis=0)

    waves = all_of(whole.at[:, pl.ds(0, (chans - 1) * 2 * width)], wave_send, wave_recv)
    waves.wait_recv()
    result = jnp.dot(whole[...], turned[...], preferred_element_type=jnp.float32)
    swapped = pltpu.roll(result, width, 1)

    def hop_copy(step):
        return pltpu.make_async_remote_copy(
            src_ref=message, dst_ref=wave_slot(me), send_sem=hop_send.at[step], recv_sem=hop_recv,
            device_id=(sector + 1 + step, me), device_id_type=MESH,
        )

    @pl.when(sends)
    def _():
        message[...] = result.astype(jnp.bfloat16)

        def go(step, carry):
            hop_copy(following - 1 - step).start()
            return carry

        lax.fori_loop(0, following, go, 0)

        def done(step, carry):
            hop_copy(step).wait_send()
            return carry

        lax.fori_loop(0, following, done, 0)

    out_ref[0] = (result - swapped)[:, :width]
    out_ref[1] = result[:, :width]
    levels.wait_send()
    waves.wait_send()
    all_of(basis.at[pl.ds(0, n // 2 * OWN // (OWN + 2)), :], ring_send, hop_recv).wait_send()
    all_of(basis.at[pl.ds(0, n // 2), :], twin_send, hop_recv).wait_send()


def local(angular, potential, point_rows, quanta, start_waves):
    chans, sectors = lax.axis_size("chan"), lax.axis_size("sector")
    points, n = angular.shape[0], angular.shape[1] * chans
    solutions, width = start_waves.shape
    vmem, hbm = pl.BlockSpec(memory_space=pltpu.VMEM), pl.BlockSpec(memory_space=pltpu.HBM)
    return pl.pallas_call(
        functools.partial(kernel, chans, sectors),
        out_shape=jax.ShapeDtypeStruct((2, solutions, width), jnp.float32),
        in_specs=[
            hbm,
            pl.BlockSpec(memory_space=pltpu.SMEM),
            hbm, hbm, hbm,
        ],
        out_specs=vmem,
        scratch_shapes=[
            pltpu.VMEM(potential.shape, jnp.float32),
            pltpu.VMEM(quanta.shape, jnp.int32),
            pltpu.VMEM(start_waves.shape, jnp.float32),
            pltpu.VMEM((n, points), jnp.bfloat16),
            pltpu.VMEM((points, n), jnp.bfloat16),
            pltpu.VMEM((2, 2 * width, n), jnp.float32),
            pltpu.VMEM((2 * width, n), jnp.bfloat16),
            pltpu.VMEM((2 * width, points), jnp.bfloat16),
            pltpu.VMEM((2 * width, points), jnp.float32),
            pltpu.VMEM((2 * n, 2 * width), jnp.bfloat16),
            pltpu.VMEM((solutions, 2 * n), jnp.bfloat16),
            pltpu.VMEM((solutions, 2 * width), jnp.bfloat16),
            pltpu.VMEM((chans, 8, 2 * width), jnp.float32),
            pltpu.VMEM((8, n), jnp.float32),
            pltpu.SemaphoreType.DMA,
            pltpu.SemaphoreType.DMA,
            pltpu.SemaphoreType.DMA,
            pltpu.SemaphoreType.DMA,
            pltpu.SemaphoreType.DMA((max(GROUPS),)),
            pltpu.SemaphoreType.DMA,
            pltpu.SemaphoreType.DMA,
            pltpu.SemaphoreType.DMA((2, OWN)),
            pltpu.SemaphoreType.DMA,
            pltpu.SemaphoreType.DMA((2, OWN // 2 + 1)),
            pltpu.SemaphoreType.DMA((4,)),
        ],
        compiler_params=pltpu.CompilerParams(
            collective_id=0, has_side_effects=True, vmem_limit_bytes=60 * 1024 * 1024
        ),
    )(angular.T, point_rows, potential, quanta, start_waves)


def solution(mesh):
    placed = (P(None, "chan"), P(), P(), P(None, "chan"), P(None, "chan"))
    return jax.shard_map(
        local, mesh=mesh, in_specs=placed, out_specs=P("sector", None, "chan"), check_vma=False
    )
```

```python
import functools

import jax
import jax.numpy as jnp
from jax import lax
from jax.experimental import pallas as pl
from jax.experimental.pallas import tpu as pltpu
from jax.sharding import PartitionSpec as P

energy = 3.5
rotor_const = 0.02
radius_first = 8.0
radius_step = 0.5
step_square = 0.08

GROUPS = (2, 3, 5, 6)
PASS_AT = (99, 5, 9, 99)
TILE = 1024
MESH = pl.DeviceIdType.MESH

SIDE = 4
STEPS = (0, -1, 1, 2)
PIECES = [(f, s, part) for f in STEPS for s in STEPS if (f, s) != (0, 0) for part in (0, 1)]
OWN = len(PIECES)
FORE, BACK, UP, DOWN = (1, 0), (-1, 0), (0, 1), (0, -1)
OWN_TO = [
    (part, toward, PIECES.index((-toward[0], -toward[1], part)))
    for turn in (0, 1)
    for toward, early in ((FORE, 0), (BACK, 1), (UP, 0), (DOWN, 1))
    for part in (early if turn == 0 else 1 - early,)
]


def sent_on(piece):
    f, s, part = piece
    result = []
    if s == 0:
        if (f, part) == (-1, 0):
            result.append((FORE, PIECES.index((2, 0, 0))))
        if (f, part) == (1, 1):
            result.append((BACK, PIECES.index((2, 0, 1))))
        result += [(UP, PIECES.index((f, -1, part))), (DOWN, PIECES.index((f, 1, part)))]
    if (s, part) == (-1, 0):
        result.append((UP, PIECES.index((f, 2, 0))))
    if (s, part) == (1, 1):
        result.append((DOWN, PIECES.index((f, 2, 1))))
    return result


FORWARD = [sent_on(piece) for piece in PIECES]
FAR_FIRST = sorted(
    [(dx, dy) for dx in STEPS for dy in STEPS if (dx, dy) != (0, 0)], key=lambda o: -abs(o[0]) - abs(o[1])
)
ORDER = [
    ("pieces", [(-1, 0, 0), (1, 0, 1), (0, -1, 0), (0, 1, 1), (-1, 0, 1), (1, 0, 0), (0, -1, 1), (0, 1, 0)]),
    ("take", [(0, 0)]),
    ("pieces", [(2, 0, 0), (2, 0, 1), (-1, -1, 0), (1, -1, 0), (-1, 1, 1), (1, 1, 1)]),
    ("take", [(-1, 0), (0, -1)]),
    ("pieces", [(0, 2, 0), (0, 2, 1), (-1, -1, 1), (1, -1, 1), (-1, 1, 0), (1, 1, 0)]),
    ("take", [(1, 0), (0, 1)]),
    ("pieces", [(2, -1, 0), (2, 1, 1)]), ("levels", 0), ("take", [(-1, -1), (1, -1)]),
    ("pieces", [(2, -1, 1), (2, 1, 0)]), ("levels", 1), ("take", [(-1, 1), (1, 1)]),
    ("pieces", [(-1, 2, 0), (-1, 2, 1)]), ("take", [(2, 0), (0, 2)]),
    ("pieces", [(1, 2, 0), (1, 2, 1)]), ("take", [(2, -1), (-1, 2)]),
    ("waves", 0), ("waves", 1), ("take", [(2, 1), (1, 2)]), ("pieces", [(2, 2, 0), (2, 2, 1)]), ("take", [(2, 2)]),
]


def pick(index, values):
    result = values[-1]
    for place in range(len(values) - 1):
        result = jnp.where(index == place, values[place], result)
    return result


def kernel(
    chans, sectors,
    mine_ref, rows_ref, pot_in, quanta_in, start_in, out_ref,
    pot_ref, quanta_ref, start_ref,
    basis, flipped, state, rounded, weighted, summed, turned,
    whole, message, terms, table, level_send, level_recv, wave_send, wave_recv, hop_send, hop_recv,
    ring_send, ring_recv, twin_send, twin_recv, load_sem,
):
    n = basis.shape[0]
    width = n // chans
    sector, me = lax.axis_index("sector"), lax.axis_index("chan")
    first_of, last_of, next_of, pass_of = [], [], [], []
    start = 0
    for index, size in enumerate(GROUPS):
        following = GROUPS[index + 1] if index + 1 < len(GROUPS) else 0
        for _ in range(size):
            first_of.append(start)
            last_of.append(start + size - 1)
            next_of.append(following)
            pass_of.append(PASS_AT[index])
        start += size
    first = pick(sector, first_of)
    last = pick(sector, last_of)
    following = pick(sector, next_of)
    pass_at = pick(sector, pass_of)
    sends = jnp.logical_and(sector == last, following > 0)
    previous = first - 1

    core, y_at, x_at = lax.rem(me, 2), lax.rem(me // 2, SIDE), me // (2 * SIDE)
    twin = me + 1 - 2 * core
    cut = n // 2
    own_rows = pl.ds(pl.multiple_of(me * width, width), width)
    loads = [
        pltpu.make_async_copy(source, place, load_sem.at[index])
        for index, (source, place) in enumerate([
            (quanta_in, quanta_ref), (start_in, start_ref), (mine_ref, basis.at[own_rows, :]), (pot_in, pot_ref),
        ])
    ]
    for load in loads:
        load.start()

    barrier = pltpu.get_barrier_semaphore()

    def greet(distance, carry):
        peer = lax.rem(me + distance, chans)
        pl.semaphore_signal(barrier, inc=1, device_id=(sector, peer), device_id_type=MESH)
        return carry

    lax.fori_loop(1, chans, greet, 0)

    @pl.when(sends)
    def _():
        def greet_next(step, carry):
            pl.semaphore_signal(barrier, inc=1, device_id=(sector + 1 + step, me), device_id_type=MESH)
            return carry

        lax.fori_loop(0, following, greet_next, 0)

    @pl.when(first > 0)
    def _():
        pl.semaphore_signal(barrier, inc=1, device_id=(previous, me), device_id_type=MESH)

    greeted = chans - 1 + jnp.where(sends, following, 0) + jnp.where(first > 0, 1, 0)
    pl.semaphore_wait(barrier, greeted)

    def level_copy(peer):
        return pltpu.make_async_remote_copy(
            src_ref=terms.at[me], dst_ref=terms.at[me],
            send_sem=level_send, recv_sem=level_recv,
            device_id=(sector, peer), device_id_type=MESH,
        )

    def wave_slot(owner):
        return whole.at[:, pl.ds(pl.multiple_of(owner * 2 * width, 2 * width), 2 * width)]

    def wave_copy(peer):
        return pltpu.make_async_remote_copy(
            src_ref=wave_slot(me), dst_ref=wave_slot(me),
            send_sem=wave_send, recv_sem=wave_recv,
            device_id=(sector, peer), device_id_type=MESH,
        )

    def to_peers(make, portion=None):
        for place, (dx, dy) in enumerate(FAR_FIRST):
            if portion in (None, place % 2):
                for side in (0, 1):
                    make(chip_of(0, dx, dy) * 2 + side).start()
        if portion != 0:
            make(twin).start()

    def chip_of(half, first_step, second_step):
        dx, dy = (first_step, second_step) if half == 0 else (second_step, first_step)
        return lax.rem(x_at + dx + SIDE, SIDE) * SIDE + lax.rem(y_at + dy + SIDE, SIDE)

    def piece(half, owner, part):
        begin, size = (0, width) if part is None else (part * (width // 2), width // 2)
        rows = pl.ds(pl.multiple_of(owner * width + begin, width // 2), size)
        return basis.at[rows, pl.ds(half * cut, cut)]

    def ring_copy(half, slot, toward, target, source=None):
        first_step, second_step, part = (0, 0, PIECES[target][2]) if slot is None else PIECES[slot]
        owner = chip_of(half, first_step, second_step) * 2 + core
        return pltpu.make_async_remote_copy(
            src_ref=piece(half, owner, part) if source is None else source,
            dst_ref=piece(half, owner, part),
            send_sem=ring_send, recv_sem=ring_recv.at[half, target],
            device_id=(sector, chip_of(half, *toward) * 2 + core), device_id_type=MESH,
        )

    def twin_copy(half, slot, side):
        first_step, second_step, _ = PIECES[slot]
        place = piece(half, chip_of(half, first_step, second_step) * 2 + side, None)
        return pltpu.make_async_remote_copy(
            src_ref=place, dst_ref=place,
            send_sem=twin_send, recv_sem=twin_recv.at[half, slot // 2],
            device_id=(sector, twin), device_id_type=MESH,
        )

    def arrived(half, slot, both):
        pltpu.make_async_remote_copy(
            src_ref=mine_ref.at[pl.ds(0, width // 2), pl.ds(0, cut)], dst_ref=piece(
                half, chip_of(half, *PIECES[slot][:2]) * 2 + core, PIECES[slot][2]
            ),
            send_sem=ring_send, recv_sem=ring_recv.at[half, slot],
            device_id=(sector, twin), device_id_type=MESH,
        ).wait_recv()
        for toward, target in FORWARD[slot]:
            ring_copy(half, slot, toward, target).start()
        if both:
            twin_copy(half, slot, core).start()

    def own_twin_copy(owner):
        place = basis.at[pl.ds(pl.multiple_of(owner * width, width), width), :]
        return pltpu.make_async_remote_copy(
            src_ref=mine_ref, dst_ref=place, send_sem=twin_send, recv_sem=twin_recv.at[0, OWN // 2],
            device_id=(sector, twin), device_id_type=MESH,
        )

    def own_part(half, part):
        return mine_ref.at[pl.ds(part * (width // 2), width // 2), pl.ds(half * cut, cut)]

    for part, toward, target in OWN_TO:
        for half in (0, 1):
            ring_copy(half, None, toward, target, own_part(half, part)).start()
    own_twin_copy(me).start()

    loads[0].wait()
    quanta = quanta_ref[...].astype(jnp.float32)
    j_values, l_values = quanta[0:1, :], quanta[1:2, :]
    a_row = 2.0 - step_square * (energy - rotor_const * j_values * (j_values + 1.0))
    b_row = step_square * (l_values * (l_values + 1.0))
    ab = jnp.concatenate([a_row, b_row, jnp.zeros((6, width), jnp.float32)], axis=0)
    lane = lax.broadcasted_iota(jnp.int32, (8, 2 * width), 1)
    half = lane // width
    terms[me] = jnp.where(half == lax.rem(me, 2), jnp.concatenate([ab, ab], axis=1), 0.0)
    loads[1].wait()

    @pl.when(first == 0)
    def _():
        waves = start_ref[...].astype(jnp.bfloat16)
        whole[:, pl.ds(pl.multiple_of(me * 2 * width, 2 * width), 2 * width)] = jnp.concatenate(
            [waves, waves], axis=1
        )

    top = 2 * sector + 1
    bottom = 2 * first
    top_row = rows_ref[top]
    loads[2].wait()
    loads[3].wait()
    weighted[pl.ds(0, width), :] = (
        basis[own_rows, :].astype(jnp.float32) * pot_ref[pl.ds(top_row, 1), :]
    ).astype(jnp.bfloat16)
    summed[...] = jnp.zeros_like(summed)

    def level_of(point, a_row, b_row):
        radius = jnp.full(a_row.shape, radius_first, jnp.float32) + radius_step * point.astype(jnp.float32)
        return a_row + b_row * (1.0 / (radius * radius))

    own_level = level_of(top, terms[me, 0:1, :], terms[me, 1:2, :])

    def take(chips):
        places, news = [], []
        for chip in chips:
            columns = pl.ds(pl.multiple_of(chip * 128, 128), 128)
            for begin in range(0, n, TILE):
                flipped[pl.ds(begin, TILE), columns] = jnp.transpose(basis[columns, pl.ds(begin, TILE)])
            places.append(columns)
        for chip, columns in zip(chips, places):
            product = jnp.dot(
                weighted[pl.ds(0, width), :], flipped[:, columns], preferred_element_type=jnp.float32
            )
            row = lax.broadcasted_iota(jnp.int32, (width, 128), 0)
            column = lax.broadcasted_iota(jnp.int32, (width, 128), 1) + chip * 128
            own = jnp.where(column == me * width + row, 1.0, 0.0)
            both = jnp.concatenate([own_level * own - step_square * product, own], axis=0)
            state[0, :, columns] = jnp.concatenate([own, jnp.zeros_like(own)], axis=0)
            state[1, :, columns] = both
            news.append(both.astype(jnp.bfloat16))
        for begin in range(0, n, TILE):
            tile = pl.ds(begin, TILE)
            total = summed[:, tile]
            for columns, both in zip(places, news):
                total += jnp.dot(both, basis[columns, tile], preferred_element_type=jnp.float32)
            summed[:, tile] = total

    handed = ([], [])
    for kind, what in ORDER:
        if kind == "pieces":
            for name in what:
                for half in (0, 1):
                    handed[half].append(name)
                    arrived(half, PIECES.index(name), name[:2] + (1 - name[2],) in handed[half])
        elif kind == "levels":
            to_peers(level_copy, what)
        elif kind == "waves":
            @pl.when(first == 0)
            def _(portion=what):
                to_peers(wave_copy, portion)
        else:
            for dx, dy in what:
                if (dx, dy) == (0, 0):
                    own_twin_copy(twin).wait_recv()
                else:
                    for half, steps_to in ((0, (dx, dy)), (1, (dy, dx))):
                        twin_copy(half, PIECES.index(steps_to + (0,)), 1 - core).wait_recv()
            take([chip_of(0, dx, dy) for dx, dy in what])

    def all_of(place, send_sem, recv_sem):
        return pltpu.make_async_remote_copy(
            src_ref=place, dst_ref=place, send_sem=send_sem, recv_sem=recv_sem,
            device_id=(sector, twin), device_id_type=MESH,
        )

    levels = all_of(terms.at[pl.ds(0, chans - 1)], level_send, level_recv)
    levels.wait_recv()

    @pl.loop(0, chans // 2)
    def _(pair):
        table[:, pl.ds(pl.multiple_of(pair * 128, 128), 128)] = terms[2 * pair] + terms[2 * pair + 1]

    steps = top - bottom + 1

    def weigh(product, point, columns):
        weighted[:, columns] = (product * pot_ref[pl.ds(rows_ref[point], 1), columns]).astype(jnp.bfloat16)

    for begin in range(0, n, TILE):
        weigh(summed[:, pl.ds(begin, TILE)], top - 1, pl.ds(begin, TILE))

    def pass_on():
        pltpu.make_async_remote_copy(
            src_ref=message, dst_ref=wave_slot(me), send_sem=hop_send.at[0], recv_sem=hop_recv,
            device_id=(previous, me), device_id_type=MESH,
        ).wait_recv()
        to_peers(wave_copy)

    def back(step, carry):
        point = top - step

        @pl.when(jnp.logical_and(step == pass_at, first > 0))
        def _():
            pass_on()

        current, other = lax.rem(step, 2), 1 - lax.rem(step, 2)
        for begin in range(0, n, TILE):
            columns = pl.ds(begin, TILE)
            product = jnp.dot(weighted[...], flipped[:, columns], preferred_element_type=jnp.float32)
            new = (
                level_of(point, table[0:1, columns], table[1:2, columns]) * state[current, :, columns]
                - state[other, :, columns] - step_square * product
            )
            state[other, :, columns] = new
            rounded[:, columns] = new.astype(jnp.bfloat16)

        @pl.when(step + 1 < steps)
        def _():
            for begin in range(0, n, TILE):
                columns = pl.ds(begin, TILE)
                weigh(
                    jnp.dot(rounded[...], basis[:, columns], preferred_element_type=jnp.float32),
                    point - 1, columns,
                )

        return carry

    lax.fori_loop(1, steps, back, 0)

    @pl.when(jnp.logical_and(steps <= pass_at, first > 0))
    def _():
        pass_on()

    newest, older = lax.rem(steps, 2), 1 - lax.rem(steps, 2)

    def differences(rows):
        return jnp.concatenate([rows[:width], rows[:width] - rows[width:]], axis=0)

    @pl.loop(0, chans // 4)
    def _(quarter):
        for part in range(2):
            pair = 2 * quarter + part
            columns = pl.ds(pl.multiple_of(pair * 128, 128), 128)
            before = differences(state[older, :, columns])
            main = differences(state[newest, :, columns]) - before
            main, before = (jnp.transpose(v.astype(jnp.bfloat16)) for v in (main, before))
            for side in range(2):
                place = pl.ds(pl.multiple_of((2 * pair + side) * 128, 128), 128)
                lines = slice(side * width, (side + 1) * width)
                turned[place, :] = jnp.concatenate([main[lines], before[lines]], axis=0)

    waves = all_of(whole.at[:, pl.ds(0, (chans - 1) * 2 * width)], wave_send, wave_recv)
    waves.wait_recv()
    result = jnp.dot(whole[...], turned[...], preferred_element_type=jnp.float32)
    swapped = pltpu.roll(result, width, 1)

    def hop_copy(step):
        return pltpu.make_async_remote_copy(
            src_ref=message, dst_ref=wave_slot(me), send_sem=hop_send.at[step], recv_sem=hop_recv,
            device_id=(sector + 1 + step, me), device_id_type=MESH,
        )

    @pl.when(sends)
    def _():
        message[...] = result.astype(jnp.bfloat16)

        def go(step, carry):
            hop_copy(following - 1 - step).start()
            return carry

        lax.fori_loop(0, following, go, 0)

        def done(step, carry):
            hop_copy(step).wait_send()
            return carry

        lax.fori_loop(0, following, done, 0)

    out_ref[0] = (result - swapped)[:, :width]
    out_ref[1] = result[:, :width]
    levels.wait_send()
    waves.wait_send()
    all_of(basis.at[pl.ds(0, n // 2 * OWN // (OWN + 2)), :], ring_send, hop_recv).wait_send()
    all_of(basis.at[pl.ds(0, n // 2), :], twin_send, hop_recv).wait_send()


def local(angular, potential, point_rows, quanta, start_waves):
    chans, sectors = lax.axis_size("chan"), lax.axis_size("sector")
    points, n = angular.shape[0], angular.shape[1] * chans
    solutions, width = start_waves.shape
    vmem, hbm = pl.BlockSpec(memory_space=pltpu.VMEM), pl.BlockSpec(memory_space=pltpu.HBM)
    return pl.pallas_call(
        functools.partial(kernel, chans, sectors),
        out_shape=jax.ShapeDtypeStruct((2, solutions, width), jnp.float32),
        in_specs=[
            hbm,
            pl.BlockSpec(memory_space=pltpu.SMEM),
            hbm, hbm, hbm,
        ],
        out_specs=vmem,
        scratch_shapes=[
            pltpu.VMEM(potential.shape, jnp.float32),
            pltpu.VMEM(quanta.shape, jnp.int32),
            pltpu.VMEM(start_waves.shape, jnp.float32),
            pltpu.VMEM((n, points), jnp.bfloat16),
            pltpu.VMEM((points, n), jnp.bfloat16),
            pltpu.VMEM((2, 2 * width, n), jnp.float32),
            pltpu.VMEM((2 * width, n), jnp.bfloat16),
            pltpu.VMEM((2 * width, points), jnp.bfloat16),
            pltpu.VMEM((2 * width, points), jnp.float32),
            pltpu.VMEM((2 * n, 2 * width), jnp.bfloat16),
            pltpu.VMEM((solutions, 2 * n), jnp.bfloat16),
            pltpu.VMEM((solutions, 2 * width), jnp.bfloat16),
            pltpu.VMEM((chans, 8, 2 * width), jnp.float32),
            pltpu.VMEM((8, n), jnp.float32),
            pltpu.SemaphoreType.DMA,
            pltpu.SemaphoreType.DMA,
            pltpu.SemaphoreType.DMA,
            pltpu.SemaphoreType.DMA,
            pltpu.SemaphoreType.DMA((max(GROUPS),)),
            pltpu.SemaphoreType.DMA,
            pltpu.SemaphoreType.DMA,
            pltpu.SemaphoreType.DMA((2, OWN)),
            pltpu.SemaphoreType.DMA,
            pltpu.SemaphoreType.DMA((2, OWN // 2 + 1)),
            pltpu.SemaphoreType.DMA((4,)),
        ],
        compiler_params=pltpu.CompilerParams(
            collective_id=0, has_side_effects=True, vmem_limit_bytes=60 * 1024 * 1024
        ),
    )(angular.T, point_rows, potential, quanta, start_waves)


def solution(mesh):
    placed = (P(None, "chan"), P(), P(), P(None, "chan"), P(None, "chan"))
    return jax.shard_map(
        local, mesh=mesh, in_specs=placed, out_specs=P("sector", None, "chan"), check_vma=False
    )
```
